32 devices in a mesh: row: 4 (over y, x), col: 8 (over z, core).
Axes of the slice: x: 2, y: 2, z: 4, core: 2. Of those that a mesh axis runs over, the one named last changes fastest.
Arguments:
- amplitudes: float32 [256, 512], P('row', 'col'), may hold values from -6 to 6
- integrals: float32 [4096, 512], P('col', 'row'), may hold values from -0.75 to 0.75
- irrep_ij: int32 [256], P('row'), may hold values from 0 to 7
- irrep_ab: int32 [4096], P('col'), may hold values from 0 to 7
- irrep_cd: int32 [512], replicated, may hold values from 0 to 7
Outputs:
- ladder: float32 [256, 4096], P('row', 'col')
The draws below stay inside these ranges and needn't reach their ends.
All inputs are finite; a program needn't handle non-finite values.
Results may differ from the reference program's by a relative error of at most 0.00014.
Values sent between devices are 32-bit elements; how exact they have to be, the bound alone decides.
A program may use at most 64 MiB of HBM per device.

```python
import jax
import jax.numpy as jnp
from jax import lax

N_IRREP = 8
IJ = 256
AB = 4096
CD = 512


def with_ends(values, stream_key, smallest, largest):
    place = [jax.random.randint(jax.random.fold_in(stream_key, axis), (), 0, length) for axis, length in enumerate(values.shape)]
    widest = values.shape.index(max(values.shape))
    next_to = place[:widest] + [(place[widest] + 1) % values.shape[widest]] + place[widest + 1:]
    return values.at[tuple(place)].set(smallest).at[tuple(next_to)].set(largest)


def steps_of(own_key, extent, cuts, smallest, top_value):
    gain = 1.0
    for dim, blocks in cuts:
        draws = jax.random.uniform(jax.random.fold_in(jax.random.fold_in(own_key, 6), dim), (blocks,), jnp.float32, smallest / len(cuts), top_value / len(cuts))
        gain = gain * jnp.repeat(jnp.exp(draws), extent[dim] // blocks).reshape((-1,) + (1,) * (len(extent) - 1 - dim))
    return gain


def normal_values(rng, extent, scale, reach, split=(), kind=jnp.bfloat16):
    drawn = scale * jax.random.normal(rng, extent, jnp.float32)
    if split:
        drawn = drawn * steps_of(rng, extent, split, -0.22, 0.18)
    return jnp.clip(drawn, -reach, reach).astype(kind)


def setup_inputs(seed: int = 0) -> dict:
    key_of = jax.random.split(jax.random.key(seed), 6)
    amplitudes = normal_values(key_of[0], (IJ, CD), 1.0, 6.0, ((0, 4), (1, 8)), jnp.float32)
    integrals = normal_values(key_of[1], (AB, CD), (CD // N_IRREP) ** -0.5, 0.75, ((0, 8), (1, 4)), jnp.float32)
    irrep_ij = with_ends(jax.random.randint(key_of[2], (IJ,), 0, N_IRREP), jax.random.fold_in(key_of[2], 1), 0, N_IRREP - 1).astype(jnp.int32)
    irrep_ab = with_ends(jax.random.randint(key_of[3], (AB,), 0, N_IRREP), jax.random.fold_in(key_of[3], 1), 0, N_IRREP - 1).astype(jnp.int32)
    irrep_cd = with_ends(jax.random.randint(key_of[4], (CD,), 0, N_IRREP), jax.random.fold_in(key_of[4], 1), 0, N_IRREP - 1).astype(jnp.int32)
    return dict(amplitudes=amplitudes, integrals=integrals, irrep_ij=irrep_ij, irrep_ab=irrep_ab, irrep_cd=irrep_cd)


def reference(amplitudes, integrals, irrep_ij, irrep_ab, irrep_cd):
    masked = jnp.where(irrep_ij[:, None] == irrep_cd[None, :], amplitudes, jnp.zeros((), amplitudes.dtype))
    summed = lax.dot_general(masked, integrals, (((1,), (1,)), ((), ())), precision=lax.Precision.HIGHEST, preferred_element_type=jnp.float32)
    return jnp.where(irrep_ij[:, None] == irrep_ab[None, :], summed, jnp.zeros((), summed.dtype))
```

```python
import functools
import math

import jax
import jax.numpy as jnp
from jax import lax
from jax.experimental import pallas as pl
from jax.experimental.pallas import tpu as pltpu
from jax.sharding import PartitionSpec as P

N_IRREP = 8
MESH = pl.DeviceIdType.MESH


def slots_for(block):
    need = block / N_IRREP + 4.0 * math.sqrt(block * (N_IRREP - 1)) / N_IRREP
    return min(-(-block // 8) * 8, 8 * math.ceil(need / 8))


def halves(x):
    high = x.astype(jnp.bfloat16)
    low = (x - high.astype(jnp.float32)).astype(jnp.bfloat16)
    return high, low


def nt_dot(a, b):
    return lax.dot_general(a, b, (((1,), (1,)), ((), ())), preferred_element_type=jnp.float32)


def selector(labels, slots):
    block = labels.shape[1]
    irreps = lax.broadcasted_iota(jnp.int32, (N_IRREP, block), 0)
    member = jnp.where(irreps == labels, 1.0, 0.0)
    before = lax.broadcasted_iota(jnp.int32, (block, block), 0) < lax.broadcasted_iota(
        jnp.int32, (block, block), 1
    )
    earlier = jnp.dot(
        member.astype(jnp.bfloat16),
        jnp.where(before, 1.0, 0.0).astype(jnp.bfloat16),
        preferred_element_type=jnp.float32,
    )
    rank = jnp.sum(member * earlier, axis=0, keepdims=True)
    place = labels * slots + rank.astype(jnp.int32)
    rows = lax.broadcasted_iota(jnp.int32, (N_IRREP * slots, block), 0)
    return jnp.where(rows == place, 1.0, 0.0).astype(jnp.bfloat16)


def pack(sel, values, labels, slots):
    high, low = halves(values)
    picked = nt_dot(
        jnp.concatenate([sel, sel], axis=1), jnp.concatenate([high, low], axis=1)
    )
    packed = jnp.zeros((slots, values.shape[0]), jnp.float32)
    for irrep in range(N_IRREP):
        packed = jnp.where(
            labels == irrep, picked[irrep * slots : (irrep + 1) * slots], packed
        )
    return packed


def kernel(
    n_row, n_col, slots, amp_ref, int_ref, ij_ref, ab_ref, cd_ref, out_ref, fits_ref,
    t_all, v_all, t_send, t_recv, v_send, v_recv,
):
    row, col = lax.axis_index("row"), lax.axis_index("col")
    per_row = n_col // n_row
    ij_rows, part = amp_ref.shape
    block = int_ref.shape[1]

    row_peers = [lax.rem(row + step, n_row) for step in range(1, n_row)]
    col_peers = [lax.rem(col + step, n_col) for step in range(1, n_col)]
    barrier = pltpu.get_barrier_semaphore()
    for peer in row_peers:
        pl.semaphore_signal(barrier, inc=1, device_id=(peer, col), device_id_type=MESH)
    for peer in col_peers:
        pl.semaphore_signal(barrier, inc=1, device_id=(row, peer), device_id_type=MESH)

    v_sel = selector(cd_ref[pl.ds(row, 1), :], slots)
    v_all[row] = pack(v_sel, int_ref[...], ab_ref[...], slots)

    pl.semaphore_wait(barrier, n_row - 1 + n_col - 1)
    copies = []
    for step, peer in enumerate(row_peers):
        copy = pltpu.make_async_remote_copy(
            src_ref=v_all.at[row], dst_ref=v_all.at[row],
            send_sem=v_send.at[step], recv_sem=v_recv.at[row],
            device_id=(peer, col), device_id_type=MESH,
        )
        copy.start()
        copies.append(copy)

    t_sel = selector(cd_ref[pl.ds(lax.div(col, per_row), 1), :], slots)
    lanes = lax.broadcasted_iota(jnp.int32, (ij_rows, block), 1)
    own = lax.div(lanes, part) == lax.rem(col, per_row)
    amps = amp_ref[...]
    spread = jnp.where(own, jnp.concatenate([amps] * per_row, axis=1), 0.0)
    t_all[col] = pack(t_sel, spread, ij_ref[...], slots)
    for step, peer in enumerate(col_peers):
        copy = pltpu.make_async_remote_copy(
            src_ref=t_all.at[col], dst_ref=t_all.at[col],
            send_sem=t_send.at[step], recv_sem=t_recv.at[col],
            device_id=(row, peer), device_id_type=MESH,
        )
        copy.start()
        copies.append(copy)

    most = jnp.zeros((n_row, 1), jnp.int32)
    for irrep in range(N_IRREP):
        count = jnp.sum(jnp.where(cd_ref[...] == irrep, 1, 0), axis=1, keepdims=True)
        most = jnp.maximum(most, count)
    fits_ref[0] = jnp.where(jnp.max(most) <= slots, 1, 0)

    wide = jnp.broadcast_to(ij_ref[...], (8, ij_rows)).astype(jnp.float32)
    ij_column = jnp.transpose(wide)[:, :1].astype(jnp.int32)
    same = ij_column == ab_ref[...]

    for peer in col_peers:
        pltpu.make_async_remote_copy(
            src_ref=t_all.at[peer], dst_ref=t_all.at[peer],
            send_sem=t_send.at[0], recv_sem=t_recv.at[peer],
            device_id=(row, peer), device_id_type=MESH,
        ).wait_recv()
    t_rows = []
    for first in range(0, n_col, per_row):
        total = t_all[first]
        for other in range(first + 1, first + per_row):
            total = total + t_all[other]
        t_rows.append(total)
    t_high, t_low = halves(jnp.transpose(jnp.concatenate(t_rows, axis=0)))
    left = jnp.concatenate([t_high, t_high, t_low], axis=1)

    for peer in row_peers:
        pltpu.make_async_remote_copy(
            src_ref=v_all.at[peer], dst_ref=v_all.at[peer],
            send_sem=v_send.at[0], recv_sem=v_recv.at[peer],
            device_id=(peer, col), device_id_type=MESH,
        ).wait_recv()
    v_high, v_low = halves(v_all[...].reshape(n_row * slots, -1))
    right = jnp.concatenate([v_high, v_low, v_high], axis=0)
    summed = jnp.dot(left, right, preferred_element_type=jnp.float32)
    out_ref[...] = jnp.where(same, summed, 0.0)
    for copy in copies:
        copy.wait_send()


def packed_ladder(n_row, n_col, amplitudes, integrals, irrep_ij, irrep_ab, irrep_cd):
    ij_rows, ab_rows = amplitudes.shape[0], integrals.shape[0]
    block = integrals.shape[1]
    slots = slots_for(block)
    vmem = pl.BlockSpec(memory_space=pltpu.VMEM)
    return pl.pallas_call(
        functools.partial(kernel, n_row, n_col, slots),
        out_shape=(
            jax.ShapeDtypeStruct((ij_rows, ab_rows), jnp.float32),
            jax.ShapeDtypeStruct((1,), jnp.int32),
        ),
        in_specs=[vmem] * 5,
        out_specs=(vmem, pl.BlockSpec(memory_space=pltpu.SMEM)),
        scratch_shapes=[
            pltpu.VMEM((n_col, slots, ij_rows), jnp.float32),
            pltpu.VMEM((n_row, slots, ab_rows), jnp.float32),
            pltpu.SemaphoreType.DMA((n_col,)),
            pltpu.SemaphoreType.DMA((n_col,)),
            pltpu.SemaphoreType.DMA((n_row,)),
            pltpu.SemaphoreType.DMA((n_row,)),
        ],
        compiler_params=pltpu.CompilerParams(
            collective_id=0, has_side_effects=True, vmem_limit_bytes=32 * 1024 * 1024
        ),
    )(
        amplitudes, integrals, irrep_ij.reshape(1, -1), irrep_ab.reshape(1, -1),
        irrep_cd.reshape(n_row, block),
    )


def dense_ladder(amplitudes, integrals, irrep_ij, irrep_ab, irrep_cd):
    gathered = lax.all_gather(amplitudes, "col", axis=1, tiled=True)
    gathered = jnp.where(irrep_ij[:, None] == irrep_cd[None, :], gathered, 0.0)
    summed = lax.dot_general(
        gathered,
        lax.all_gather(integrals, "row", axis=1, tiled=True),
        (((1,), (1,)), ((), ())),
        precision=lax.Precision.HIGHEST,
        preferred_element_type=jnp.float32,
    )
    return jnp.where(irrep_ij[:, None] == irrep_ab[None, :], summed, 0.0)


def solution(mesh):
    n_row, n_col = mesh.shape["row"], mesh.shape["col"]

    def body(*arrays):
        if n_col % n_row:
            return dense_ladder(*arrays)
        ladder, fits = packed_ladder(n_row, n_col, *arrays)
        return lax.cond(
            fits[0] == 1, lambda ladder, *_: ladder, lambda _, *rest: dense_ladder(*rest),
            ladder, *arrays,
        )

    in_specs = (P("row", "col"), P("col", "row"), P("row"), P("col"), P())
    return jax.shard_map(
        body, mesh=mesh, in_specs=in_specs, out_specs=P("row", "col"), check_vma=False
    )
```

```python
import functools
import math

import jax
import jax.numpy as jnp
from jax import lax
from jax.experimental import pallas as pl
from jax.experimental.pallas import tpu as pltpu
from jax.sharding import PartitionSpec as P

N_IRREP = 8
MESH = pl.DeviceIdType.MESH


def slots_for(block):
    need = block / N_IRREP + 4.0 * math.sqrt(block * (N_IRREP - 1)) / N_IRREP
    return min(-(-block // 8) * 8, 8 * math.ceil(need / 8))


def halves(x):
    high = x.astype(jnp.bfloat16)
    low = (x - high.astype(jnp.float32)).astype(jnp.bfloat16)
    return high, low


def nt_dot(a, b):
    return lax.dot_general(a, b, (((1,), (1,)), ((), ())), preferred_element_type=jnp.float32)


def selector(labels, slots):
    block = labels.shape[1]
    irreps = lax.broadcasted_iota(jnp.int32, (N_IRREP, block), 0)
    member = jnp.where(irreps == labels, 1.0, 0.0)
    before = lax.broadcasted_iota(jnp.int32, (block, block), 0) < lax.broadcasted_iota(
        jnp.int32, (block, block), 1
    )
    earlier = jnp.dot(
        member.astype(jnp.bfloat16),
        jnp.where(before, 1.0, 0.0).astype(jnp.bfloat16),
        preferred_element_type=jnp.float32,
    )
    rank = jnp.sum(member * earlier, axis=0, keepdims=True)
    place = labels * slots + rank.astype(jnp.int32)
    rows = lax.broadcasted_iota(jnp.int32, (N_IRREP * slots, block), 0)
    return jnp.where(rows == place, 1.0, 0.0).astype(jnp.bfloat16)


def pack(sel, values, labels, slots):
    high, low = halves(values)
    picked = nt_dot(
        jnp.concatenate([sel, sel], axis=1), jnp.concatenate([high, low], axis=1)
    )
    packed = jnp.zeros((slots, values.shape[0]), jnp.float32)
    for irrep in range(N_IRREP):
        packed = jnp.where(
            labels == irrep, picked[irrep * slots : (irrep + 1) * slots], packed
        )
    return packed


def kernel(
    n_row, n_col, slots, amp_ref, int_ref, ij_ref, ab_ref, cd_ref, out_ref, fits_ref,
    t_all, v_all, t_send, t_recv, v_send, v_recv,
):
    row, col = lax.axis_index("row"), lax.axis_index("col")
    per_row = n_col // n_row
    ij_rows, part = amp_ref.shape
    block = int_ref.shape[1]

    row_peers = [lax.rem(row + step, n_row) for step in range(1, n_row)]
    col_peers = [lax.rem(col + step, n_col) for step in range(1, n_col)]
    barrier = pltpu.get_barrier_semaphore()
    for peer in row_peers:
        pl.semaphore_signal(barrier, inc=1, device_id=(peer, col), device_id_type=MESH)
    for peer in col_peers:
        pl.semaphore_signal(barrier, inc=1, device_id=(row, peer), device_id_type=MESH)

    v_sel = selector(cd_ref[pl.ds(row, 1), :], slots)
    v_all[row] = pack(v_sel, int_ref[...], ab_ref[...], slots)

    pl.semaphore_wait(barrier, n_row - 1 + n_col - 1)
    copies = []
    for step, peer in enumerate(row_peers):
        copy = pltpu.make_async_remote_copy(
            src_ref=v_all.at[row], dst_ref=v_all.at[row],
            send_sem=v_send.at[step], recv_sem=v_recv.at[row],
            device_id=(peer, col), device_id_type=MESH,
        )
        copy.start()
        copies.append(copy)

    t_sel = selector(cd_ref[pl.ds(lax.div(col, per_row), 1), :], slots)
    lanes = lax.broadcasted_iota(jnp.int32, (ij_rows, block), 1)
    own = lax.div(lanes, part) == lax.rem(col, per_row)
    amps = amp_ref[...]
    spread = jnp.where(own, jnp.concatenate([amps] * per_row, axis=1), 0.0)
    t_all[col] = pack(t_sel, spread, ij_ref[...], slots)
    for step, peer in enumerate(col_peers):
        copy = pltpu.make_async_remote_copy(
            src_ref=t_all.at[col], dst_ref=t_all.at[col],
            send_sem=t_send.at[step], recv_sem=t_recv.at[col],
            device_id=(row, peer), device_id_type=MESH,
        )
        copy.start()
        copies.append(copy)

    most = jnp.zeros((n_row, 1), jnp.int32)
    for irrep in range(N_IRREP):
        count = jnp.sum(jnp.where(cd_ref[...] == irrep, 1, 0), axis=1, keepdims=True)
        most = jnp.maximum(most, count)
    fits_ref[0] = jnp.where(jnp.max(most) <= slots, 1, 0)

    wide = jnp.broadcast_to(ij_ref[...], (8, ij_rows)).astype(jnp.float32)
    ij_column = jnp.transpose(wide)[:, :1].astype(jnp.int32)
    same = ij_column == ab_ref[...]

    for peer in col_peers:
        pltpu.make_async_remote_copy(
            src_ref=t_all.at[peer], dst_ref=t_all.at[peer],
            send_sem=t_send.at[0], recv_sem=t_recv.at[peer],
            device_id=(row, peer), device_id_type=MESH,
        ).wait_recv()
    t_rows = []
    for first in range(0, n_col, per_row):
        total = t_all[first]
        for other in range(first + 1, first + per_row):
            total = total + t_all[other]
        t_rows.append(total)
    t_high, t_low = halves(jnp.transpose(jnp.concatenate(t_rows, axis=0)))
    left = jnp.concatenate([t_high, t_high, t_low], axis=1)

    for peer in row_peers:
        pltpu.make_async_remote_copy(
            src_ref=v_all.at[peer], dst_ref=v_all.at[peer],
            send_sem=v_send.at[0], recv_sem=v_recv.at[peer],
            device_id=(peer, col), device_id_type=MESH,
        ).wait_recv()
    v_high, v_low = halves(v_all[...].reshape(n_row * slots, -1))
    right = jnp.concatenate([v_high, v_low, v_high], axis=0)
    summed = jnp.dot(left, right, preferred_element_type=jnp.float32)
    out_ref[...] = jnp.where(same, summed, 0.0)
    for copy in copies:
        copy.wait_send()


def packed_ladder(n_row, n_col, amplitudes, integrals, irrep_ij, irrep_ab, irrep_cd):
    ij_rows, ab_rows = amplitudes.shape[0], integrals.shape[0]
    block = integrals.shape[1]
    slots = slots_for(block)
    vmem = pl.BlockSpec(memory_space=pltpu.VMEM)
    return pl.pallas_call(
        functools.partial(kernel, n_row, n_col, slots),
        out_shape=(
            jax.ShapeDtypeStruct((ij_rows, ab_rows), jnp.float32),
            jax.ShapeDtypeStruct((1,), jnp.int32),
        ),
        in_specs=[vmem] * 5,
        out_specs=(vmem, pl.BlockSpec(memory_space=pltpu.SMEM)),
        scratch_shapes=[
            pltpu.VMEM((n_col, slots, ij_rows), jnp.float32),
            pltpu.VMEM((n_row, slots, ab_rows), jnp.float32),
            pltpu.SemaphoreType.DMA((n_col,)),
            pltpu.SemaphoreType.DMA((n_col,)),
            pltpu.SemaphoreType.DMA((n_row,)),
            pltpu.SemaphoreType.DMA((n_row,)),
        ],
        compiler_params=pltpu.CompilerParams(
            collective_id=0, has_side_effects=True, vmem_limit_bytes=32 * 1024 * 1024
        ),
    )(
        amplitudes, integrals, irrep_ij.reshape(1, -1), irrep_ab.reshape(1, -1),
        irrep_cd.reshape(n_row, block),
    )


def gather_kernel(n_row, n_col, amp_ref, int_ref, t_all, v_all, t_send, t_recv, v_send, v_recv, own):
    row, col = lax.axis_index("row"), lax.axis_index("col")
    barrier = pltpu.get_barrier_semaphore()

    def with_row(step):
        return (lax.rem(row + step, n_row), col)

    def with_col(step):
        return (row, lax.rem(col + step, n_col))

    for peer_of, peers in ((with_row, n_row), (with_col, n_col)):

        @pl.loop(1, peers)
        def _(step):
            pl.semaphore_signal(barrier, inc=1, device_id=peer_of(step), device_id_type=MESH)

    kept = [
        pltpu.make_async_copy(int_ref, v_all.at[row], own.at[0]),
        pltpu.make_async_copy(amp_ref, t_all.at[col], own.at[1]),
    ]
    for copy in kept:
        copy.start()
    pl.semaphore_wait(barrier, n_row - 1 + n_col - 1)

    def v_copy(step, source):
        return pltpu.make_async_remote_copy(
            src_ref=int_ref, dst_ref=v_all.at[source],
            send_sem=v_send.at[step], recv_sem=v_recv.at[source],
            device_id=with_row(step), device_id_type=MESH,
        )

    def t_copy(step, source):
        return pltpu.make_async_remote_copy(
            src_ref=amp_ref, dst_ref=t_all.at[source],
            send_sem=t_send.at[step], recv_sem=t_recv.at[source],
            device_id=with_col(step), device_id_type=MESH,
        )

    for copy_of, me, peers in ((v_copy, row, n_row), (t_copy, col, n_col)):

        @pl.loop(1, peers)
        def _(step):
            copy_of(step, me).start()

    for copy_of, me, peers in ((v_copy, row, n_row), (t_copy, col, n_col)):

        @pl.loop(1, peers)
        def _(step):
            copy_of(step, me).wait_send()
            copy_of(step, lax.rem(me + step, peers)).wait_recv()

    for copy in kept:
        copy.wait()


def dense_ladder(n_row, n_col, amplitudes, integrals, irrep_ij, irrep_ab, irrep_cd):
    vmem = pl.BlockSpec(memory_space=pltpu.VMEM)
    t_all, v_all = pl.pallas_call(
        functools.partial(gather_kernel, n_row, n_col),
        out_shape=(
            jax.ShapeDtypeStruct((n_col,) + amplitudes.shape, amplitudes.dtype),
            jax.ShapeDtypeStruct((n_row,) + integrals.shape, integrals.dtype),
        ),
        in_specs=[vmem] * 2,
        out_specs=(vmem, vmem),
        scratch_shapes=[
            pltpu.SemaphoreType.DMA((n_col,)),
            pltpu.SemaphoreType.DMA((n_col,)),
            pltpu.SemaphoreType.DMA((n_row,)),
            pltpu.SemaphoreType.DMA((n_row,)),
            pltpu.SemaphoreType.DMA((2,)),
        ],
        compiler_params=pltpu.CompilerParams(
            collective_id=1, has_side_effects=True, vmem_limit_bytes=32 * 1024 * 1024
        ),
    )(amplitudes, integrals)
    amps = jnp.swapaxes(t_all, 0, 1).reshape(amplitudes.shape[0], -1)
    ints = jnp.swapaxes(v_all, 0, 1).reshape(integrals.shape[0], -1)
    masked = jnp.where(irrep_ij[:, None] == irrep_cd[None, :], amps, 0.0)
    summed = lax.dot_general(
        masked, ints, (((1,), (1,)), ((), ())),
        precision=lax.Precision.HIGHEST, preferred_element_type=jnp.float32,
    )
    return jnp.where(irrep_ij[:, None] == irrep_ab[None, :], summed, 0.0)


def solution(mesh):
    n_row, n_col = mesh.shape["row"], mesh.shape["col"]

    def body(*arrays):
        if n_col % n_row:
            return dense_ladder(n_row, n_col, *arrays)
        ladder, fits = packed_ladder(n_row, n_col, *arrays)
        return lax.cond(
            fits[0] == 1, lambda ladder, *_: ladder, lambda _, *rest: dense_ladder(n_row, n_col, *rest),
            ladder, *arrays,
        )

    in_specs = (P("row", "col"), P("col", "row"), P("row"), P("col"), P())
    return jax.shard_map(
        body, mesh=mesh, in_specs=in_specs, out_specs=P("row", "col"), check_vma=False
    )
```

```python
import functools
import math

import jax
import jax.numpy as jnp
from jax import lax
from jax.experimental import pallas as pl
from jax.experimental.pallas import tpu as pltpu
from jax.sharding import PartitionSpec as P

N_IRREP = 8
MESH = pl.DeviceIdType.MESH


def slots_for(block):
    need = block / N_IRREP + 4.0 * math.sqrt(block * (N_IRREP - 1)) / N_IRREP
    return min(-(-block // 8) * 8, 8 * math.ceil(need / 8))


def halves(x):
    high = x.astype(jnp.bfloat16)
    low = (x - high.astype(jnp.float32)).astype(jnp.bfloat16)
    return high, low


def nt_dot(a, b):
    return lax.dot_general(a, b, (((1,), (1,)), ((), ())), preferred_element_type=jnp.float32)


def selector(labels, slots):
    block = labels.shape[1]
    irreps = lax.broadcasted_iota(jnp.int32, (N_IRREP, block), 0)
    member = jnp.where(irreps == labels, 1.0, 0.0)
    before = lax.broadcasted_iota(jnp.int32, (block, block), 0) < lax.broadcasted_iota(
        jnp.int32, (block, block), 1
    )
    earlier = jnp.dot(
        member.astype(jnp.bfloat16),
        jnp.where(before, 1.0, 0.0).astype(jnp.bfloat16),
        preferred_element_type=jnp.float32,
    )
    rank = jnp.sum(member * earlier, axis=0, keepdims=True)
    place = labels * slots + rank.astype(jnp.int32)
    rows = lax.broadcasted_iota(jnp.int32, (N_IRREP * slots, block), 0)
    return jnp.where(rows == place, 1.0, 0.0).astype(jnp.bfloat16)


def pack(sel, values, labels, slots):
    high, low = halves(values)
    picked = nt_dot(
        jnp.concatenate([sel, sel], axis=1), jnp.concatenate([high, low], axis=1)
    )
    packed = jnp.zeros((slots, values.shape[0]), jnp.float32)
    for irrep in range(N_IRREP):
        packed = jnp.where(
            labels == irrep, picked[irrep * slots : (irrep + 1) * slots], packed
        )
    return packed


def kernel(
    n_row, n_col, slots, amp_hbm, int_hbm, ij_hbm, ab_hbm, cd_hbm, out_ref, fits_ref,
    amp_ref, int_ref, ij_ref, ab_ref, cd_ref, t_half, t_all, v_all,
    load, h_send, h_recv, t_send, t_recv, v_send, v_recv,
):
    row, col = lax.axis_index("row"), lax.axis_index("col")
    per_row = n_col // n_row
    ij_rows, part = amp_ref.shape
    block = int_ref.shape[1]
    n_z = n_col // 2
    z, core = lax.div(col, 2), lax.rem(col, 2)
    sibling = (row, 2 * z + 1 - core)
    below, above = (row, col - 2), (row, col + 2)

    barrier = pltpu.get_barrier_semaphore()

    def greet(device):
        pl.semaphore_signal(barrier, inc=1, device_id=device, device_id_type=MESH)

    row_peers = [lax.rem(row + step, n_row) for step in range(1, n_row)]
    for peer in row_peers:
        greet((peer, col))
    greet(sibling)
    pl.when(z > 0)(lambda: greet(below))
    pl.when(z < n_z - 1)(lambda: greet(above))

    loads = [
        pltpu.make_async_copy(source, target, load.at[place])
        for place, (source, target) in enumerate(
            ((cd_hbm, cd_ref), (ij_hbm, ij_ref), (amp_hbm, amp_ref), (ab_hbm, ab_ref), (int_hbm, int_ref))
        )
    ]
    for copy in loads:
        copy.start()
    for copy in loads[:3]:
        copy.wait()

    t_sel = selector(cd_ref[pl.ds(lax.div(col, per_row), 1), :], slots)
    amps = amp_ref[...]
    if per_row > 1:
        lanes = lax.broadcasted_iota(jnp.int32, (ij_rows, block), 1)
        own = lax.div(lanes, part) == lax.rem(col, per_row)
        amps = jnp.where(own, jnp.concatenate([amps] * per_row, axis=1), 0.0)
    t_half[core] = pack(t_sel, amps, ij_ref[...], slots)

    v_sel = selector(cd_ref[pl.ds(row, 1), :], slots)
    for copy in loads[3:]:
        copy.wait()
    v_all[row] = pack(v_sel, int_ref[...], ab_ref[...], slots)

    ends = jnp.where(z > 0, 1, 0) + jnp.where(z < n_z - 1, 1, 0)
    pl.semaphore_wait(barrier, n_row + ends)

    def half_copy(which):
        return pltpu.make_async_remote_copy(
            src_ref=t_half.at[which], dst_ref=t_half.at[which],
            send_sem=h_send, recv_sem=h_recv, device_id=sibling, device_id_type=MESH,
        )

    half_copy(core).start()
    copies = []
    for step, peer in reversed(list(enumerate(row_peers))):
        copy = pltpu.make_async_remote_copy(
            src_ref=v_all.at[row], dst_ref=v_all.at[row],
            send_sem=v_send.at[step], recv_sem=v_recv.at[row],
            device_id=(peer, col), device_id_type=MESH,
        )
        copy.start()
        copies.append(copy)

    most = jnp.zeros((n_row, 1), jnp.int32)
    for irrep in range(N_IRREP):
        count = jnp.sum(jnp.where(cd_ref[...] == irrep, 1, 0), axis=1, keepdims=True)
        most = jnp.maximum(most, count)
    fits_ref[0] = jnp.where(jnp.max(most) <= slots, 1, 0)
    wide = jnp.broadcast_to(ij_ref[...], (8, ij_rows)).astype(jnp.float32)
    ij_column = jnp.transpose(wide)[:, :1].astype(jnp.int32)
    same = ij_column == ab_ref[...]

    half_copy(1 - core).wait_recv()
    if per_row == 2:
        t_all[z, 0] = t_half[0] + t_half[1]
    else:
        t_all[z, 0] = t_half[0]
        t_all[z, 1] = t_half[1]

    def t_copy(origin, up):
        return pltpu.make_async_remote_copy(
            src_ref=t_all.at[origin], dst_ref=t_all.at[origin],
            send_sem=t_send.at[up, origin], recv_sem=t_recv.at[origin],
            device_id=above if up else below, device_id_type=MESH,
        )

    def passes(step, up):
        origin = z - step if up else z + step
        held = origin >= 0 if up else origin < n_z
        onward = z < n_z - 1 if up else z > 0
        return origin, held, jnp.logical_and(held, onward)

    for step in range(n_z):
        for up in (1, 0):
            origin, held, goes = passes(step, up)
            if step:
                pl.when(held)(lambda: t_copy(origin, up).wait_recv())
            pl.when(goes)(lambda: t_copy(origin, up).start())

    groups = 2 // per_row
    t_rows = [t_all[place, group] for place in range(n_z) for group in range(groups)]
    t_high, t_low = halves(jnp.transpose(jnp.concatenate(t_rows, axis=0)))
    left = jnp.concatenate([t_high, t_high, t_low], axis=1)

    for peer in row_peers:
        pltpu.make_async_remote_copy(
            src_ref=v_all.at[peer], dst_ref=v_all.at[peer],
            send_sem=v_send.at[0], recv_sem=v_recv.at[peer],
            device_id=(peer, col), device_id_type=MESH,
        ).wait_recv()
    v_high, v_low = halves(v_all[...].reshape(n_row * slots, -1))
    right = jnp.concatenate([v_high, v_low, v_high], axis=0)
    summed = jnp.dot(left, right, preferred_element_type=jnp.float32)
    out_ref[...] = jnp.where(same, summed, 0.0)

    half_copy(core).wait_send()
    for copy in copies:
        copy.wait_send()
    for step in range(n_z):
        for up in (1, 0):
            origin, _, goes = passes(step, up)
            pl.when(goes)(lambda: t_copy(origin, up).wait_send())


def packed_ladder(n_row, n_col, amplitudes, integrals, irrep_ij, irrep_ab, irrep_cd):
    ij_rows, ab_rows = amplitudes.shape[0], integrals.shape[0]
    block = integrals.shape[1]
    slots = slots_for(block)
    vmem = pl.BlockSpec(memory_space=pltpu.VMEM)
    operands = (
        amplitudes, integrals, irrep_ij.reshape(1, -1), irrep_ab.reshape(1, -1),
        irrep_cd.reshape(n_row, block),
    )
    return pl.pallas_call(
        functools.partial(kernel, n_row, n_col, slots),
        out_shape=(
            jax.ShapeDtypeStruct((ij_rows, ab_rows), jnp.float32),
            jax.ShapeDtypeStruct((1,), jnp.int32),
        ),
        in_specs=[pl.BlockSpec(memory_space=pltpu.HBM)] * 5,
        out_specs=(vmem, pl.BlockSpec(memory_space=pltpu.SMEM)),
        scratch_shapes=[pltpu.VMEM(array.shape, array.dtype) for array in operands] + [
            pltpu.VMEM((2, slots, ij_rows), jnp.float32),
            pltpu.VMEM((n_col // 2, 2 * n_row // n_col, slots, ij_rows), jnp.float32),
            pltpu.VMEM((n_row, slots, ab_rows), jnp.float32),
            pltpu.SemaphoreType.DMA((5,)),
            pltpu.SemaphoreType.DMA,
            pltpu.SemaphoreType.DMA,
            pltpu.SemaphoreType.DMA((2, n_col // 2)),
            pltpu.SemaphoreType.DMA((n_col // 2,)),
            pltpu.SemaphoreType.DMA((n_row,)),
            pltpu.SemaphoreType.DMA((n_row,)),
        ],
        compiler_params=pltpu.CompilerParams(
            collective_id=0, has_side_effects=True, vmem_limit_bytes=32 * 1024 * 1024
        ),
    )(*operands)


def gather_kernel(
    n_row, n_col, amp_ref, int_ref, ij_ref, ab_ref, cd_ref, t_all, v_all, ij_out, ab_out, cd_out,
    t_send, t_recv, v_send, v_recv, own,
):
    row, col = lax.axis_index("row"), lax.axis_index("col")
    barrier = pltpu.get_barrier_semaphore()

    def with_row(step):
        return (lax.rem(row + step, n_row), col)

    def with_col(step):
        return (row, lax.rem(col + step, n_col))

    for peer_of, peers in ((with_row, n_row), (with_col, n_col)):

        @pl.loop(1, peers)
        def _(step):
            pl.semaphore_signal(barrier, inc=1, device_id=peer_of(step), device_id_type=MESH)

    kept = [
        pltpu.make_async_copy(int_ref, v_all.at[row], own.at[0]),
        pltpu.make_async_copy(amp_ref, t_all.at[col], own.at[1]),
        pltpu.make_async_copy(ij_ref, ij_out, own.at[2]),
        pltpu.make_async_copy(ab_ref, ab_out, own.at[3]),
        pltpu.make_async_copy(cd_ref, cd_out, own.at[4]),
    ]
    for copy in kept:
        copy.start()
    pl.semaphore_wait(barrier, n_row - 1 + n_col - 1)

    def v_copy(step, source):
        return pltpu.make_async_remote_copy(
            src_ref=int_ref, dst_ref=v_all.at[source],
            send_sem=v_send.at[step], recv_sem=v_recv.at[source],
            device_id=with_row(step), device_id_type=MESH,
        )

    def t_copy(step, source):
        return pltpu.make_async_remote_copy(
            src_ref=amp_ref, dst_ref=t_all.at[source],
            send_sem=t_send.at[step], recv_sem=t_recv.at[source],
            device_id=with_col(step), device_id_type=MESH,
        )

    for copy_of, me, peers in ((v_copy, row, n_row), (t_copy, col, n_col)):

        @pl.loop(1, peers)
        def _(step):
            copy_of(step, me).start()

    for copy_of, me, peers in ((v_copy, row, n_row), (t_copy, col, n_col)):

        @pl.loop(1, peers)
        def _(step):
            copy_of(step, me).wait_send()
            copy_of(step, lax.rem(me + step, peers)).wait_recv()

    for copy in kept:
        copy.wait()


def dense_ladder(n_row, n_col, amplitudes, integrals, irrep_ij, irrep_ab, irrep_cd):
    vmem = pl.BlockSpec(memory_space=pltpu.VMEM)
    labels = (irrep_ij.reshape(1, -1), irrep_ab.reshape(1, -1), irrep_cd.reshape(n_row, -1))
    t_all, v_all, irrep_ij, irrep_ab, irrep_cd = pl.pallas_call(
        functools.partial(gather_kernel, n_row, n_col),
        out_shape=(
            jax.ShapeDtypeStruct((n_col,) + amplitudes.shape, amplitudes.dtype),
            jax.ShapeDtypeStruct((n_row,) + integrals.shape, integrals.dtype),
        ) + tuple(jax.ShapeDtypeStruct(label.shape, label.dtype) for label in labels),
        in_specs=[pl.BlockSpec(memory_space=pltpu.HBM)] * 5,
        out_specs=(vmem,) * 5,
        scratch_shapes=[
            pltpu.SemaphoreType.DMA((n_col,)),
            pltpu.SemaphoreType.DMA((n_col,)),
            pltpu.SemaphoreType.DMA((n_row,)),
            pltpu.SemaphoreType.DMA((n_row,)),
            pltpu.SemaphoreType.DMA((5,)),
        ],
        compiler_params=pltpu.CompilerParams(
            collective_id=1, has_side_effects=True, vmem_limit_bytes=32 * 1024 * 1024
        ),
    )(amplitudes, integrals, *labels)
    irrep_ij, irrep_ab, irrep_cd = (label.reshape(-1) for label in (irrep_ij, irrep_ab, irrep_cd))
    amps = jnp.swapaxes(t_all, 0, 1).reshape(amplitudes.shape[0], -1)
    ints = jnp.swapaxes(v_all, 0, 1).reshape(integrals.shape[0], -1)
    masked = jnp.where(irrep_ij[:, None] == irrep_cd[None, :], amps, 0.0)
    summed = lax.dot_general(
        masked, ints, (((1,), (1,)), ((), ())),
        precision=lax.Precision.HIGHEST, preferred_element_type=jnp.float32,
    )
    return jnp.where(irrep_ij[:, None] == irrep_ab[None, :], summed, 0.0)


def solution(mesh):
    n_row, n_col = mesh.shape["row"], mesh.shape["col"]

    def body(*arrays):
        if n_col not in (n_row, 2 * n_row) or n_col % 2:
            return dense_ladder(n_row, n_col, *arrays)
        ladder, fits = packed_ladder(n_row, n_col, *arrays)
        return lax.cond(
            fits[0] == 1, lambda ladder, *_: ladder, lambda _, *rest: dense_ladder(n_row, n_col, *rest),
            ladder, *arrays,
        )

    in_specs = (P("row", "col"), P("col", "row"), P("row"), P("col"), P())
    return jax.shard_map(
        body, mesh=mesh, in_specs=in_specs, out_specs=P("row", "col"), check_vma=False
    )
```

```python
import functools
import math

import jax
import jax.numpy as jnp
from jax import lax
from jax.experimental import pallas as pl
from jax.experimental.pallas import tpu as pltpu
from jax.sharding import PartitionSpec as P

N_IRREP = 8
MESH = pl.DeviceIdType.MESH


def slots_for(block):
    need = block / N_IRREP + 4.0 * math.sqrt(block * (N_IRREP - 1)) / N_IRREP
    return min(-(-block // 8) * 8, 8 * math.ceil(need / 8))


def halves(x):
    high = x.astype(jnp.bfloat16)
    low = (x - high.astype(jnp.float32)).astype(jnp.bfloat16)
    return high, low


def nt_dot(a, b):
    return lax.dot_general(a, b, (((1,), (1,)), ((), ())), preferred_element_type=jnp.float32)


def selector(labels, slots):
    block = labels.shape[1]
    irreps = lax.broadcasted_iota(jnp.int32, (N_IRREP, block), 0)
    member = jnp.where(irreps == labels, 1.0, 0.0)
    before = lax.broadcasted_iota(jnp.int32, (block, block), 0) < lax.broadcasted_iota(
        jnp.int32, (block, block), 1
    )
    earlier = jnp.dot(
        member.astype(jnp.bfloat16),
        jnp.where(before, 1.0, 0.0).astype(jnp.bfloat16),
        preferred_element_type=jnp.float32,
    )
    rank = jnp.sum(member * earlier, axis=0, keepdims=True)
    place = labels * slots + rank.astype(jnp.int32)
    rows = lax.broadcasted_iota(jnp.int32, (N_IRREP * slots, block), 0)
    return jnp.where(rows == place, 1.0, 0.0).astype(jnp.bfloat16)


def pack(sel, values, labels, slots):
    high, low = halves(values)
    picked = nt_dot(
        jnp.concatenate([sel, sel], axis=1), jnp.concatenate([high, low], axis=1)
    )
    packed = jnp.zeros((slots, values.shape[0]), jnp.float32)
    for irrep in range(N_IRREP):
        packed = jnp.where(
            labels == irrep, picked[irrep * slots : (irrep + 1) * slots], packed
        )
    return packed


def kernel(
    n_row, n_col, slots, amp_hbm, int_hbm, ij_hbm, ab_hbm, cd_hbm, out_ref, fits_ref,
    amp_ref, int_ref, ij_ref, ab_ref, cd_ref, t_all, v_all,
    load, t_send, t_recv, v_send, v_recv,
):
    row, col = lax.axis_index("row"), lax.axis_index("col")
    per_row = n_col // n_row
    ij_rows, part = amp_ref.shape
    block = int_ref.shape[1]
    odd = lax.rem(col, 2) == 1

    barrier = pltpu.get_barrier_semaphore()

    def greet(*device):
        pl.semaphore_signal(barrier, inc=1, device_id=device, device_id_type=MESH)

    row_peers = [lax.rem(row + step, n_row) for step in range(1, n_row)]
    for peer in row_peers:
        greet(peer, col)
    for step in range(1, n_col):
        pl.when(col + step < n_col)(lambda: greet(row, col + step))
    pl.when(odd)(lambda: greet(row, col - 1))

    loads = [
        pltpu.make_async_copy(source, target, load.at[place])
        for place, (source, target) in enumerate(
            ((cd_hbm, cd_ref), (ij_hbm, ij_ref), (amp_hbm, amp_ref), (ab_hbm, ab_ref), (int_hbm, int_ref))
        )
    ]
    for copy in loads:
        copy.start()
    for copy in loads[:3]:
        copy.wait()

    t_sel = selector(cd_ref[pl.ds(lax.div(col, per_row), 1), :], slots)
    amps = amp_ref[...]
    if per_row > 1:
        lanes = lax.broadcasted_iota(jnp.int32, (ij_rows, block), 1)
        own = lax.div(lanes, part) == lax.rem(col, per_row)
        amps = jnp.where(own, jnp.concatenate([amps] * per_row, axis=1), 0.0)
    t_all[col] = pack(t_sel, amps, ij_ref[...], slots)

    v_sel = selector(cd_ref[pl.ds(row, 1), :], slots)
    for copy in loads[3:]:
        copy.wait()
    v_all[row] = pack(v_sel, int_ref[...], ab_ref[...], slots)

    pl.semaphore_wait(barrier, n_row - 1 + col + jnp.where(odd, 0, 1))

    def t_copy(origin, peer):
        return pltpu.make_async_remote_copy(
            src_ref=t_all.at[origin], dst_ref=t_all.at[origin],
            send_sem=t_send.at[peer], recv_sem=t_recv.at[origin],
            device_id=(row, peer), device_id_type=MESH,
        )

    for step in reversed(range(1, n_col)):
        pl.when(col >= step)(lambda: t_copy(col, col - step).start())
    pl.when(jnp.logical_not(odd))(lambda: t_copy(col, col + 1).start())
    copies = []
    for step, peer in reversed(list(enumerate(row_peers))):
        copy = pltpu.make_async_remote_copy(
            src_ref=v_all.at[row], dst_ref=v_all.at[row],
            send_sem=v_send.at[step], recv_sem=v_recv.at[row],
            device_id=(peer, col), device_id_type=MESH,
        )
        copy.start()
        copies.append(copy)

    most = jnp.zeros((n_row, 1), jnp.int32)
    for irrep in range(N_IRREP):
        count = jnp.sum(jnp.where(cd_ref[...] == irrep, 1, 0), axis=1, keepdims=True)
        most = jnp.maximum(most, count)
    fits_ref[0] = jnp.where(jnp.max(most) <= slots, 1, 0)
    wide = jnp.broadcast_to(ij_ref[...], (8, ij_rows)).astype(jnp.float32)
    ij_column = jnp.transpose(wide)[:, :1].astype(jnp.int32)
    same = ij_column == ab_ref[...]

    for step in range(1, n_col):

        @pl.when(col + step < n_col)
        def _():
            t_copy(col + step, col).wait_recv()
            if step == 1:
                pl.when(odd)(lambda: t_copy(col, col + 1).start())
            else:
                t_copy(col, col + step).start()

    for step in range(1, n_col):
        pl.when(col >= step)(lambda: t_copy(col - step, col).wait_recv())
    t_rows = []
    for first in range(0, n_col, per_row):
        total = t_all[first]
        for other in range(first + 1, first + per_row):
            total = total + t_all[other]
        t_rows.append(total)
    t_high, t_low = halves(jnp.transpose(jnp.concatenate(t_rows, axis=0)))
    left = jnp.concatenate([t_high, t_high, t_low], axis=1)

    for peer in row_peers:
        pltpu.make_async_remote_copy(
            src_ref=v_all.at[peer], dst_ref=v_all.at[peer],
            send_sem=v_send.at[0], recv_sem=v_recv.at[peer],
            device_id=(peer, col), device_id_type=MESH,
        ).wait_recv()
    v_high, v_low = halves(v_all[...].reshape(n_row * slots, -1))
    right = jnp.concatenate([v_high, v_low, v_high], axis=0)
    summed = jnp.dot(left, right, preferred_element_type=jnp.float32)
    out_ref[...] = jnp.where(same, summed, 0.0)

    for copy in copies:
        copy.wait_send()
    for step in range(1, n_col):
        pl.when(col >= step)(lambda: t_copy(col, col - step).wait_send())
        pl.when(col + step < n_col)(lambda: t_copy(col, col + step).wait_send())


def packed_ladder(n_row, n_col, amplitudes, integrals, irrep_ij, irrep_ab, irrep_cd):
    ij_rows, ab_rows = amplitudes.shape[0], integrals.shape[0]
    block = integrals.shape[1]
    slots = slots_for(block)
    vmem = pl.BlockSpec(memory_space=pltpu.VMEM)
    operands = (amplitudes, integrals, irrep_ij, irrep_ab, irrep_cd)
    return pl.pallas_call(
        functools.partial(kernel, n_row, n_col, slots),
        out_shape=(
            jax.ShapeDtypeStruct((ij_rows, ab_rows), jnp.float32),
            jax.ShapeDtypeStruct((1,), jnp.int32),
        ) + tuple(jax.ShapeDtypeStruct(array.shape, array.dtype) for array in operands),
        in_specs=[pl.BlockSpec(memory_space=pltpu.HBM)] * 5,
        out_specs=(vmem, pl.BlockSpec(memory_space=pltpu.SMEM)) + (vmem,) * 5,
        scratch_shapes=[
            pltpu.VMEM((n_col, slots, ij_rows), jnp.float32),
            pltpu.VMEM((n_row, slots, ab_rows), jnp.float32),
            pltpu.SemaphoreType.DMA((5,)),
            pltpu.SemaphoreType.DMA((n_col,)),
            pltpu.SemaphoreType.DMA((n_col,)),
            pltpu.SemaphoreType.DMA((n_row,)),
            pltpu.SemaphoreType.DMA((n_row,)),
        ],
        compiler_params=pltpu.CompilerParams(
            collective_id=0, has_side_effects=True, vmem_limit_bytes=32 * 1024 * 1024
        ),
    )(*operands)


def gather_kernel(
    n_row, n_col, amp_ref, int_ref, ij_ref, ab_ref, cd_ref, t_all, v_all, ij_out, ab_out, cd_out,
    t_send, t_recv, v_send, v_recv, own,
):
    row, col = lax.axis_index("row"), lax.axis_index("col")
    barrier = pltpu.get_barrier_semaphore()

    def with_row(step):
        return (lax.rem(row + step, n_row), col)

    def with_col(step):
        return (row, lax.rem(col + step, n_col))

    for peer_of, peers in ((with_row, n_row), (with_col, n_col)):

        @pl.loop(1, peers)
        def _(step):
            pl.semaphore_signal(barrier, inc=1, device_id=peer_of(step), device_id_type=MESH)

    kept = [
        pltpu.make_async_copy(int_ref, v_all.at[row], own.at[0]),
        pltpu.make_async_copy(amp_ref, t_all.at[col], own.at[1]),
        pltpu.make_async_copy(ij_ref, ij_out, own.at[2]),
        pltpu.make_async_copy(ab_ref, ab_out, own.at[3]),
        pltpu.make_async_copy(cd_ref, cd_out, own.at[4]),
    ]
    for copy in kept:
        copy.start()
    pl.semaphore_wait(barrier, n_row - 1 + n_col - 1)

    def v_copy(step, source):
        return pltpu.make_async_remote_copy(
            src_ref=int_ref, dst_ref=v_all.at[source],
            send_sem=v_send.at[step], recv_sem=v_recv.at[source],
            device_id=with_row(step), device_id_type=MESH,
        )

    def t_copy(step, source):
        return pltpu.make_async_remote_copy(
            src_ref=amp_ref, dst_ref=t_all.at[source],
            send_sem=t_send.at[step], recv_sem=t_recv.at[source],
            device_id=with_col(step), device_id_type=MESH,
        )

    for copy_of, me, peers in ((v_copy, row, n_row), (t_copy, col, n_col)):

        @pl.loop(1, peers)
        def _(step):
            copy_of(step, me).start()

    for copy_of, me, peers in ((v_copy, row, n_row), (t_copy, col, n_col)):

        @pl.loop(1, peers)
        def _(step):
            copy_of(step, me).wait_send()
            copy_of(step, lax.rem(me + step, peers)).wait_recv()

    for copy in kept:
        copy.wait()


def dense_ladder(n_row, n_col, amplitudes, integrals, irrep_ij, irrep_ab, irrep_cd):
    vmem = pl.BlockSpec(memory_space=pltpu.VMEM)
    labels = (irrep_ij, irrep_ab, irrep_cd)
    t_all, v_all, irrep_ij, irrep_ab, irrep_cd = pl.pallas_call(
        functools.partial(gather_kernel, n_row, n_col),
        out_shape=(
            jax.ShapeDtypeStruct((n_col,) + amplitudes.shape, amplitudes.dtype),
            jax.ShapeDtypeStruct((n_row,) + integrals.shape, integrals.dtype),
        ) + tuple(jax.ShapeDtypeStruct(label.shape, label.dtype) for label in labels),
        in_specs=[pl.BlockSpec(memory_space=pltpu.HBM)] * 5,
        out_specs=(vmem,) * 5,
        scratch_shapes=[
            pltpu.SemaphoreType.DMA((n_col,)),
            pltpu.SemaphoreType.DMA((n_col,)),
            pltpu.SemaphoreType.DMA((n_row,)),
            pltpu.SemaphoreType.DMA((n_row,)),
            pltpu.SemaphoreType.DMA((5,)),
        ],
        compiler_params=pltpu.CompilerParams(
            collective_id=1, has_side_effects=True, vmem_limit_bytes=32 * 1024 * 1024
        ),
    )(amplitudes, integrals, *labels)
    irrep_ij, irrep_ab, irrep_cd = (label.reshape(-1) for label in (irrep_ij, irrep_ab, irrep_cd))
    amps = jnp.swapaxes(t_all, 0, 1).reshape(amplitudes.shape[0], -1)
    ints = jnp.swapaxes(v_all, 0, 1).reshape(integrals.shape[0], -1)
    masked = jnp.where(irrep_ij[:, None] == irrep_cd[None, :], amps, 0.0)
    summed = lax.dot_general(
        masked, ints, (((1,), (1,)), ((), ())),
        precision=lax.Precision.HIGHEST, preferred_element_type=jnp.float32,
    )
    return jnp.where(irrep_ij[:, None] == irrep_ab[None, :], summed, 0.0)


def solution(mesh):
    n_row, n_col = mesh.shape["row"], mesh.shape["col"]

    def body(*arrays):
        amplitudes, integrals, irrep_ij, irrep_ab, irrep_cd = arrays
        arrays = (
            amplitudes, integrals, irrep_ij.reshape(1, -1), irrep_ab.reshape(1, -1),
            irrep_cd.reshape(n_row, -1),
        )
        if n_col % n_row or n_col % 2:
            return dense_ladder(n_row, n_col, *arrays)
        ladder, fits, *arrays = packed_ladder(n_row, n_col, *arrays)
        return lax.cond(
            fits[0] == 1,
            lambda ladder, *_: ladder, lambda _, *rest: dense_ladder(n_row, n_col, *rest),
            ladder, *arrays,
        )

    in_specs = (P("row", "col"), P("col", "row"), P("row"), P("col"), P())
    return jax.shard_map(
        body, mesh=mesh, in_specs=in_specs, out_specs=P("row", "col"), check_vma=False
    )
```

```python
import functools
import math

import jax
import jax.numpy as jnp
from jax import lax
from jax.experimental import pallas as pl
from jax.experimental.pallas import tpu as pltpu
from jax.sharding import PartitionSpec as P

N_IRREP = 8
MESH = pl.DeviceIdType.MESH


def slots_for(block):
    need = block / N_IRREP + 4.0 * math.sqrt(block * (N_IRREP - 1)) / N_IRREP
    return min(-(-block // 8) * 8, 8 * math.ceil(need / 8))


def halves(x):
    high = x.astype(jnp.bfloat16)
    low = (x - high.astype(jnp.float32)).astype(jnp.bfloat16)
    return high, low


def nt_dot(a, b):
    return lax.dot_general(a, b, (((1,), (1,)), ((), ())), preferred_element_type=jnp.float32)


def selector(labels, slots):
    block = labels.shape[1]
    irreps = lax.broadcasted_iota(jnp.int32, (N_IRREP, block), 0)
    member = jnp.where(irreps == labels, 1.0, 0.0)
    before = lax.broadcasted_iota(jnp.int32, (block, block), 0) < lax.broadcasted_iota(
        jnp.int32, (block, block), 1
    )
    earlier = jnp.dot(
        member.astype(jnp.bfloat16),
        jnp.where(before, 1.0, 0.0).astype(jnp.bfloat16),
        preferred_element_type=jnp.float32,
    )
    rank = jnp.sum(member * earlier, axis=0, keepdims=True)
    place = labels * slots + rank.astype(jnp.int32)
    rows = lax.broadcasted_iota(jnp.int32, (N_IRREP * slots, block), 0)
    return jnp.where(rows == place, 1.0, 0.0).astype(jnp.bfloat16)


def pack(sel, values, labels, slots):
    high, low = halves(values)
    picked = nt_dot(
        jnp.concatenate([sel, sel], axis=1), jnp.concatenate([high, low], axis=1)
    )
    packed = jnp.zeros((slots, values.shape[0]), jnp.float32)
    for irrep in range(N_IRREP):
        packed = jnp.where(
            labels == irrep, picked[irrep * slots : (irrep + 1) * slots], packed
        )
    return packed


def kernel(
    n_row, n_col, slots, amp_hbm, int_hbm, ij_hbm, ab_hbm, cd_hbm, out_ref, fits_ref,
    amp_ref, int_ref, ij_ref, ab_ref, cd_ref, t_all, v_all,
    load, t_send, t_recv, v_send, v_recv,
):
    row, col = lax.axis_index("row"), lax.axis_index("col")
    per_row = n_col // n_row
    ij_rows, part = amp_ref.shape
    block = int_ref.shape[1]
    odd = lax.rem(col, 2) == 1

    barrier = pltpu.get_barrier_semaphore()

    def greet(*device):
        pl.semaphore_signal(barrier, inc=1, device_id=device, device_id_type=MESH)

    row_peers = [lax.rem(row + step, n_row) for step in range(1, n_row)]
    for peer in row_peers:
        greet(peer, col)
    for step in range(1, n_col):
        pl.when(col + step < n_col)(lambda: greet(row, col + step))
    pl.when(odd)(lambda: greet(row, col - 1))

    loads = [
        pltpu.make_async_copy(source, target, load.at[place])
        for place, (source, target) in enumerate(
            ((cd_hbm, cd_ref), (ij_hbm, ij_ref), (amp_hbm, amp_ref), (ab_hbm, ab_ref), (int_hbm, int_ref))
        )
    ]
    for copy in loads:
        copy.start()
    for copy in loads[:3]:
        copy.wait()

    t_sel = selector(cd_ref[pl.ds(lax.div(col, per_row), 1), :], slots)
    amps = amp_ref[...]
    if per_row > 1:
        lanes = lax.broadcasted_iota(jnp.int32, (ij_rows, block), 1)
        own = lax.div(lanes, part) == lax.rem(col, per_row)
        amps = jnp.where(own, jnp.concatenate([amps] * per_row, axis=1), 0.0)
    t_all[col] = pack(t_sel, amps, ij_ref[...], slots)

    v_sel = selector(cd_ref[pl.ds(row, 1), :], slots)
    for copy in loads[3:]:
        copy.wait()
    v_all[row] = pack(v_sel, int_ref[...], ab_ref[...], slots)

    pl.semaphore_wait(barrier, n_row - 1 + col + jnp.where(odd, 0, 1))

    def t_copy(origin, peer):
        return pltpu.make_async_remote_copy(
            src_ref=t_all.at[origin], dst_ref=t_all.at[origin],
            send_sem=t_send.at[peer], recv_sem=t_recv.at[origin],
            device_id=(row, peer), device_id_type=MESH,
        )

    for step in reversed(range(1, n_col)):
        pl.when(col >= step)(lambda: t_copy(col, col - step).start())
    pl.when(jnp.logical_not(odd))(lambda: t_copy(col, col + 1).start())
    copies = []
    for step, peer in reversed(list(enumerate(row_peers))):
        copy = pltpu.make_async_remote_copy(
            src_ref=v_all.at[row], dst_ref=v_all.at[row],
            send_sem=v_send.at[step], recv_sem=v_recv.at[row],
            device_id=(peer, col), device_id_type=MESH,
        )
        copy.start()
        copies.append(copy)

    most = jnp.zeros((n_row, 1), jnp.int32)
    for irrep in range(N_IRREP):
        count = jnp.sum(jnp.where(cd_ref[...] == irrep, 1, 0), axis=1, keepdims=True)
        most = jnp.maximum(most, count)
    fits_ref[0] = jnp.where(jnp.max(most) <= slots, 1, 0)
    wide = jnp.broadcast_to(ij_ref[...], (8, ij_rows)).astype(jnp.float32)
    ij_column = jnp.transpose(wide)[:, :1].astype(jnp.int32)
    same = ij_column == ab_ref[...]

    for step in range(1, n_col):

        @pl.when(col + step < n_col)
        def _():
            t_copy(col + step, col).wait_recv()
            if step == 1:
                pl.when(odd)(lambda: t_copy(col, col + 1).start())
            else:
                t_copy(col, col + step).start()

    for step in range(1, n_col):
        pl.when(col >= step)(lambda: t_copy(col - step, col).wait_recv())
    t_rows = []
    for first in range(0, n_col, per_row):
        total = t_all[first]
        for other in range(first + 1, first + per_row):
            total = total + t_all[other]
        t_rows.append(total)
    t_high, t_low = halves(jnp.transpose(jnp.concatenate(t_rows, axis=0)))
    left = jnp.concatenate([t_high, t_high, t_low], axis=1)

    for peer in row_peers:
        pltpu.make_async_remote_copy(
            src_ref=v_all.at[peer], dst_ref=v_all.at[peer],
            send_sem=v_send.at[0], recv_sem=v_recv.at[peer],
            device_id=(peer, col), device_id_type=MESH,
        ).wait_recv()
    v_high, v_low = halves(v_all[...].reshape(n_row * slots, -1))
    right = jnp.concatenate([v_high, v_low, v_high], axis=0)
    summed = jnp.dot(left, right, preferred_element_type=jnp.float32)
    out_ref[...] = jnp.where(same, summed, 0.0)

    for copy in copies:
        copy.wait_send()
    for step in range(1, n_col):
        pl.when(col >= step)(lambda: t_copy(col, col - step).wait_send())
        pl.when(col + step < n_col)(lambda: t_copy(col, col + step).wait_send())


def packed_ladder(n_row, n_col, amplitudes, integrals, irrep_ij, irrep_ab, irrep_cd):
    ij_rows, ab_rows = amplitudes.shape[0], integrals.shape[0]
    block = integrals.shape[1]
    slots = slots_for(block)
    vmem = pl.BlockSpec(memory_space=pltpu.VMEM)
    operands = (amplitudes, integrals, irrep_ij, irrep_ab, irrep_cd)
    return pl.pallas_call(
        functools.partial(kernel, n_row, n_col, slots),
        out_shape=(
            jax.ShapeDtypeStruct((ij_rows, ab_rows), jnp.float32),
            jax.ShapeDtypeStruct((1,), jnp.int32),
        ) + tuple(jax.ShapeDtypeStruct(array.shape, array.dtype) for array in operands),
        in_specs=[pl.BlockSpec(memory_space=pltpu.HBM)] * 5,
        out_specs=(vmem, pl.BlockSpec(memory_space=pltpu.SMEM)) + (vmem,) * 5,
        scratch_shapes=[
            pltpu.VMEM((n_col, slots, ij_rows), jnp.float32),
            pltpu.VMEM((n_row, slots, ab_rows), jnp.float32),
            pltpu.SemaphoreType.DMA((5,)),
            pltpu.SemaphoreType.DMA((n_col,)),
            pltpu.SemaphoreType.DMA((n_col,)),
            pltpu.SemaphoreType.DMA((n_row,)),
            pltpu.SemaphoreType.DMA((n_row,)),
        ],
        compiler_params=pltpu.CompilerParams(
            collective_id=0, has_side_effects=True, vmem_limit_bytes=60 * 1024 * 1024
        ),
    )(*operands)


def gather_kernel(
    n_row, n_col, amp_ref, int_ref, ij_ref, ab_ref, cd_ref, t_all, v_all, ij_out, ab_out, cd_out,
    t_send, t_recv, v_send, v_recv, own,
):
    row, col = lax.axis_index("row"), lax.axis_index("col")
    barrier = pltpu.get_barrier_semaphore()

    def with_row(step):
        return (lax.rem(row + step, n_row), col)

    def with_col(step):
        return (row, lax.rem(col + step, n_col))

    for peer_of, peers in ((with_row, n_row), (with_col, n_col)):

        @pl.loop(1, peers)
        def _(step):
            pl.semaphore_signal(barrier, inc=1, device_id=peer_of(step), device_id_type=MESH)

    kept = [
        pltpu.make_async_copy(int_ref, v_all.at[row], own.at[0]),
        pltpu.make_async_copy(amp_ref, t_all.at[col], own.at[1]),
        pltpu.make_async_copy(ij_ref, ij_out, own.at[2]),
        pltpu.make_async_copy(ab_ref, ab_out, own.at[3]),
        pltpu.make_async_copy(cd_ref, cd_out, own.at[4]),
    ]
    for copy in kept:
        copy.start()
    pl.semaphore_wait(barrier, n_row - 1 + n_col - 1)

    def v_copy(step, source):
        return pltpu.make_async_remote_copy(
            src_ref=int_ref, dst_ref=v_all.at[source],
            send_sem=v_send.at[step], recv_sem=v_recv.at[source],
            device_id=with_row(step), device_id_type=MESH,
        )

    def t_copy(step, source):
        return pltpu.make_async_remote_copy(
            src_ref=amp_ref, dst_ref=t_all.at[source],
            send_sem=t_send.at[step], recv_sem=t_recv.at[source],
            device_id=with_col(step), device_id_type=MESH,
        )

    for copy_of, me, peers in ((v_copy, row, n_row), (t_copy, col, n_col)):

        @pl.loop(1, peers)
        def _(step):
            copy_of(step, me).start()

    for copy_of, me, peers in ((v_copy, row, n_row), (t_copy, col, n_col)):

        @pl.loop(1, peers)
        def _(step):
            copy_of(step, me).wait_send()
            copy_of(step, lax.rem(me + step, peers)).wait_recv()

    for copy in kept:
        copy.wait()


def dense_ladder(n_row, n_col, amplitudes, integrals, irrep_ij, irrep_ab, irrep_cd):
    vmem = pl.BlockSpec(memory_space=pltpu.VMEM)
    labels = (irrep_ij, irrep_ab, irrep_cd)
    t_all, v_all, irrep_ij, irrep_ab, irrep_cd = pl.pallas_call(
        functools.partial(gather_kernel, n_row, n_col),
        out_shape=(
            jax.ShapeDtypeStruct((n_col,) + amplitudes.shape, amplitudes.dtype),
            jax.ShapeDtypeStruct((n_row,) + integrals.shape, integrals.dtype),
        ) + tuple(jax.ShapeDtypeStruct(label.shape, label.dtype) for label in labels),
        in_specs=[pl.BlockSpec(memory_space=pltpu.HBM)] * 5,
        out_specs=(vmem,) * 5,
        scratch_shapes=[
            pltpu.SemaphoreType.DMA((n_col,)),
            pltpu.SemaphoreType.DMA((n_col,)),
            pltpu.SemaphoreType.DMA((n_row,)),
            pltpu.SemaphoreType.DMA((n_row,)),
            pltpu.SemaphoreType.DMA((5,)),
        ],
        compiler_params=pltpu.CompilerParams(
            collective_id=1, has_side_effects=True, vmem_limit_bytes=32 * 1024 * 1024
        ),
    )(amplitudes, integrals, *labels)
    irrep_ij, irrep_ab, irrep_cd = (label.reshape(-1) for label in (irrep_ij, irrep_ab, irrep_cd))
    amps = jnp.swapaxes(t_all, 0, 1).reshape(amplitudes.shape[0], -1)
    ints = jnp.swapaxes(v_all, 0, 1).reshape(integrals.shape[0], -1)
    masked = jnp.where(irrep_ij[:, None] == irrep_cd[None, :], amps, 0.0)
    summed = lax.dot_general(
        masked, ints, (((1,), (1,)), ((), ())),
        precision=lax.Precision.HIGHEST, preferred_element_type=jnp.float32,
    )
    return jnp.where(irrep_ij[:, None] == irrep_ab[None, :], summed, 0.0)


def solution(mesh):
    n_row, n_col = mesh.shape["row"], mesh.shape["col"]

    def body(*arrays):
        amplitudes, integrals, irrep_ij, irrep_ab, irrep_cd = arrays
        arrays = (
            amplitudes, integrals, irrep_ij.reshape(1, -1), irrep_ab.reshape(1, -1),
            irrep_cd.reshape(n_row, -1),
        )
        if n_col % n_row or n_col % 2:
            return dense_ladder(n_row, n_col, *arrays)
        ladder, fits, *arrays = packed_ladder(n_row, n_col, *arrays)
        return lax.cond(
            fits[0] == 1,
            lambda ladder, *_: ladder, lambda _, *rest: dense_ladder(n_row, n_col, *rest),
            ladder, *arrays,
        )

    in_specs = (P("row", "col"), P("col", "row"), P("row"), P("col"), P())
    return jax.shard_map(
        body, mesh=mesh, in_specs=in_specs, out_specs=P("row", "col"), check_vma=False
    )
```

```python
import functools
import math

import jax
import jax.numpy as jnp
from jax import lax
from jax.experimental import pallas as pl
from jax.experimental.pallas import tpu as pltpu
from jax.sharding import PartitionSpec as P

N_IRREP = 8
MESH = pl.DeviceIdType.MESH


def slots_for(block):
    need = block / N_IRREP + 4.0 * math.sqrt(block * (N_IRREP - 1)) / N_IRREP
    return min(-(-block // 8) * 8, 8 * math.ceil(need / 8))


def halves(x):
    high = x.astype(jnp.bfloat16)
    low = (x - high.astype(jnp.float32)).astype(jnp.bfloat16)
    return high, low


def nt_dot(a, b):
    return lax.dot_general(a, b, (((1,), (1,)), ((), ())), preferred_element_type=jnp.float32)


def selector(labels, slots):
    block = labels.shape[1]
    irreps = lax.broadcasted_iota(jnp.int32, (N_IRREP, block), 0)
    member = jnp.where(irreps == labels, 1.0, 0.0)
    before = lax.broadcasted_iota(jnp.int32, (block, block), 0) < lax.broadcasted_iota(
        jnp.int32, (block, block), 1
    )
    earlier = jnp.dot(
        member.astype(jnp.bfloat16),
        jnp.where(before, 1.0, 0.0).astype(jnp.bfloat16),
        preferred_element_type=jnp.float32,
    )
    rank = jnp.sum(member * earlier, axis=0, keepdims=True)
    place = labels * slots + rank.astype(jnp.int32)
    rows = lax.broadcasted_iota(jnp.int32, (N_IRREP * slots, block), 0)
    return jnp.where(rows == place, 1.0, 0.0).astype(jnp.bfloat16)


def pack(sel, values, labels, slots):
    high, low = halves(values)
    picked = nt_dot(
        jnp.concatenate([sel, sel], axis=1), jnp.concatenate([high, low], axis=1)
    )
    packed = jnp.zeros((slots, values.shape[0]), jnp.float32)
    for irrep in range(N_IRREP):
        packed = jnp.where(
            labels == irrep, picked[irrep * slots : (irrep + 1) * slots], packed
        )
    return packed


def kernel(
    n_row, n_col, slots, amp_hbm, int_hbm, ij_hbm, ab_hbm, cd_hbm, out_ref, fits_ref,
    amp_ref, int_ref, ij_ref, ab_ref, cd_ref, t_all, v_all,
    load, ready, t_send, t_recv, v_send, v_recv,
):
    row, col = lax.axis_index("row"), lax.axis_index("col")
    per_row = n_col // n_row
    ij_rows, part = amp_ref.shape
    block = int_ref.shape[1]
    odd = lax.rem(col, 2) == 1

    barrier = pltpu.get_barrier_semaphore()

    def greet(*device):
        pl.semaphore_signal(barrier, inc=1, device_id=device, device_id_type=MESH)

    row_peers = [lax.rem(row + step, n_row) for step in range(1, n_row)]
    for peer in row_peers:
        greet(peer, col)
    for step in range(1, n_col):
        pl.when(col + step < n_col)(lambda: greet(row, col + step))
    pl.when(odd)(lambda: greet(row, col - 1))

    loads = [
        pltpu.make_async_copy(source, target, load.at[place])
        for place, (source, target) in enumerate(
            ((cd_hbm, cd_ref), (ij_hbm, ij_ref), (amp_hbm, amp_ref), (ab_hbm, ab_ref), (int_hbm, int_ref))
        )
    ]
    for copy in loads:
        copy.start()
    pl.semaphore_wait(barrier, n_row - 1 + col + jnp.where(odd, 0, 1))

    def tell(peer):
        pl.semaphore_signal(
            ready.at[col], inc=1, device_id=(row, peer), device_id_type=MESH
        )

    for step in reversed(range(1, n_col)):
        far = jnp.logical_or(step > 1, jnp.logical_not(odd))
        pl.when(jnp.logical_and(col >= step, far))(lambda: tell(col - step))
    for copy in loads[:3]:
        copy.wait()

    t_sel = selector(cd_ref[pl.ds(lax.div(col, per_row), 1), :], slots)
    amps = amp_ref[...]
    if per_row > 1:
        lanes = lax.broadcasted_iota(jnp.int32, (ij_rows, block), 1)
        own = lax.div(lanes, part) == lax.rem(col, per_row)
        amps = jnp.where(own, jnp.concatenate([amps] * per_row, axis=1), 0.0)
    t_all[col] = pack(t_sel, amps, ij_ref[...], slots)

    def t_copy(origin, peer):
        return pltpu.make_async_remote_copy(
            src_ref=t_all.at[origin], dst_ref=t_all.at[origin],
            send_sem=t_send.at[peer], recv_sem=t_recv.at[origin],
            device_id=(row, peer), device_id_type=MESH,
        )

    for step in reversed(range(1, n_col)):
        pl.when(col >= step)(lambda: t_copy(col, col - step).start())
    pl.when(jnp.logical_not(odd))(lambda: t_copy(col, col + 1).start())

    v_sel = selector(cd_ref[pl.ds(row, 1), :], slots)
    for copy in loads[3:]:
        copy.wait()
    v_all[row] = pack(v_sel, int_ref[...], ab_ref[...], slots)

    copies = []
    for step, peer in reversed(list(enumerate(row_peers))):
        copy = pltpu.make_async_remote_copy(
            src_ref=v_all.at[row], dst_ref=v_all.at[row],
            send_sem=v_send.at[step], recv_sem=v_recv.at[row],
            device_id=(peer, col), device_id_type=MESH,
        )
        copy.start()
        copies.append(copy)

    for step in range(1, n_col):
        far = jnp.logical_or(step > 1, odd)

        @pl.when(jnp.logical_and(col + step < n_col, far))
        def _():
            pl.semaphore_wait(ready.at[col + step], 1)
            t_copy(col, col + step).start()

    most = jnp.zeros((n_row, 1), jnp.int32)
    for irrep in range(N_IRREP):
        count = jnp.sum(jnp.where(cd_ref[...] == irrep, 1, 0), axis=1, keepdims=True)
        most = jnp.maximum(most, count)
    fits_ref[0] = jnp.where(jnp.max(most) <= slots, 1, 0)
    wide = jnp.broadcast_to(ij_ref[...], (8, ij_rows)).astype(jnp.float32)
    ij_column = jnp.transpose(wide)[:, :1].astype(jnp.int32)
    same = ij_column == ab_ref[...]

    for step in range(1, n_col):
        pl.when(col + step < n_col)(lambda: t_copy(col + step, col).wait_recv())
    for step in range(1, n_col):
        pl.when(col >= step)(lambda: t_copy(col - step, col).wait_recv())
    t_rows = []
    for first in range(0, n_col, per_row):
        total = t_all[first]
        for other in range(first + 1, first + per_row):
            total = total + t_all[other]
        t_rows.append(total)
    t_high, t_low = halves(jnp.transpose(jnp.concatenate(t_rows, axis=0)))
    left = jnp.concatenate([t_high, t_high, t_low], axis=1)

    for peer in row_peers:
        pltpu.make_async_remote_copy(
            src_ref=v_all.at[peer], dst_ref=v_all.at[peer],
            send_sem=v_send.at[0], recv_sem=v_recv.at[peer],
            device_id=(peer, col), device_id_type=MESH,
        ).wait_recv()
    v_high, v_low = halves(v_all[...].reshape(n_row * slots, -1))
    right = jnp.concatenate([v_high, v_low, v_high], axis=0)
    summed = jnp.dot(left, right, preferred_element_type=jnp.float32)
    out_ref[...] = jnp.where(same, summed, 0.0)

    for copy in copies:
        copy.wait_send()
    for step in range(1, n_col):
        pl.when(col >= step)(lambda: t_copy(col, col - step).wait_send())
        pl.when(col + step < n_col)(lambda: t_copy(col, col + step).wait_send())


def packed_ladder(n_row, n_col, amplitudes, integrals, irrep_ij, irrep_ab, irrep_cd):
    ij_rows, ab_rows = amplitudes.shape[0], integrals.shape[0]
    block = integrals.shape[1]
    slots = slots_for(block)
    vmem = pl.BlockSpec(memory_space=pltpu.VMEM)
    operands = (amplitudes, integrals, irrep_ij, irrep_ab, irrep_cd)
    return pl.pallas_call(
        functools.partial(kernel, n_row, n_col, slots),
        out_shape=(
            jax.ShapeDtypeStruct((ij_rows, ab_rows), jnp.float32),
            jax.ShapeDtypeStruct((1,), jnp.int32),
        ) + tuple(jax.ShapeDtypeStruct(array.shape, array.dtype) for array in operands),
        in_specs=[pl.BlockSpec(memory_space=pltpu.HBM)] * 5,
        out_specs=(vmem, pl.BlockSpec(memory_space=pltpu.SMEM)) + (vmem,) * 5,
        scratch_shapes=[
            pltpu.VMEM((n_col, slots, ij_rows), jnp.float32),
            pltpu.VMEM((n_row, slots, ab_rows), jnp.float32),
            pltpu.SemaphoreType.DMA((5,)),
            pltpu.SemaphoreType.REGULAR((n_col,)),
            pltpu.SemaphoreType.DMA((n_col,)),
            pltpu.SemaphoreType.DMA((n_col,)),
            pltpu.SemaphoreType.DMA((n_row,)),
            pltpu.SemaphoreType.DMA((n_row,)),
        ],
        compiler_params=pltpu.CompilerParams(
            collective_id=0, has_side_effects=True, vmem_limit_bytes=60 * 1024 * 1024
        ),
    )(*operands)


def gather_kernel(
    n_row, n_col, amp_ref, int_ref, ij_ref, ab_ref, cd_ref, t_all, v_all, ij_out, ab_out, cd_out,
    t_send, t_recv, v_send, v_recv, own,
):
    row, col = lax.axis_index("row"), lax.axis_index("col")
    barrier = pltpu.get_barrier_semaphore()

    def with_row(step):
        return (lax.rem(row + step, n_row), col)

    def with_col(step):
        return (row, lax.rem(col + step, n_col))

    for peer_of, peers in ((with_row, n_row), (with_col, n_col)):

        @pl.loop(1, peers)
        def _(step):
            pl.semaphore_signal(barrier, inc=1, device_id=peer_of(step), device_id_type=MESH)

    kept = [
        pltpu.make_async_copy(int_ref, v_all.at[row], own.at[0]),
        pltpu.make_async_copy(amp_ref, t_all.at[col], own.at[1]),
        pltpu.make_async_copy(ij_ref, ij_out, own.at[2]),
        pltpu.make_async_copy(ab_ref, ab_out, own.at[3]),
        pltpu.make_async_copy(cd_ref, cd_out, own.at[4]),
    ]
    for copy in kept:
        copy.start()
    pl.semaphore_wait(barrier, n_row - 1 + n_col - 1)

    def v_copy(step, source):
        return pltpu.make_async_remote_copy(
            src_ref=int_ref, dst_ref=v_all.at[source],
            send_sem=v_send.at[step], recv_sem=v_recv.at[source],
            device_id=with_row(step), device_id_type=MESH,
        )

    def t_copy(step, source):
        return pltpu.make_async_remote_copy(
            src_ref=amp_ref, dst_ref=t_all.at[source],
            send_sem=t_send.at[step], recv_sem=t_recv.at[source],
            device_id=with_col(step), device_id_type=MESH,
        )

    for copy_of, me, peers in ((v_copy, row, n_row), (t_copy, col, n_col)):

        @pl.loop(1, peers)
        def _(step):
            copy_of(step, me).start()

    for copy_of, me, peers in ((v_copy, row, n_row), (t_copy, col, n_col)):

        @pl.loop(1, peers)
        def _(step):
            copy_of(step, me).wait_send()
            copy_of(step, lax.rem(me + step, peers)).wait_recv()

    for copy in kept:
        copy.wait()


def dense_ladder(n_row, n_col, amplitudes, integrals, irrep_ij, irrep_ab, irrep_cd):
    vmem = pl.BlockSpec(memory_space=pltpu.VMEM)
    labels = (irrep_ij, irrep_ab, irrep_cd)
    t_all, v_all, irrep_ij, irrep_ab, irrep_cd = pl.pallas_call(
        functools.partial(gather_kernel, n_row, n_col),
        out_shape=(
            jax.ShapeDtypeStruct((n_col,) + amplitudes.shape, amplitudes.dtype),
            jax.ShapeDtypeStruct((n_row,) + integrals.shape, integrals.dtype),
        ) + tuple(jax.ShapeDtypeStruct(label.shape, label.dtype) for label in labels),
        in_specs=[pl.BlockSpec(memory_space=pltpu.HBM)] * 5,
        out_specs=(vmem,) * 5,
        scratch_shapes=[
            pltpu.SemaphoreType.DMA((n_col,)),
            pltpu.SemaphoreType.DMA((n_col,)),
            pltpu.SemaphoreType.DMA((n_row,)),
            pltpu.SemaphoreType.DMA((n_row,)),
            pltpu.SemaphoreType.DMA((5,)),
        ],
        compiler_params=pltpu.CompilerParams(
            collective_id=1, has_side_effects=True, vmem_limit_bytes=32 * 1024 * 1024
        ),
    )(amplitudes, integrals, *labels)
    irrep_ij, irrep_ab, irrep_cd = (label.reshape(-1) for label in (irrep_ij, irrep_ab, irrep_cd))
    amps = jnp.swapaxes(t_all, 0, 1).reshape(amplitudes.shape[0], -1)
    ints = jnp.swapaxes(v_all, 0, 1).reshape(integrals.shape[0], -1)
    masked = jnp.where(irrep_ij[:, None] == irrep_cd[None, :], amps, 0.0)
    summed = lax.dot_general(
        masked, ints, (((1,), (1,)), ((), ())),
        precision=lax.Precision.HIGHEST, preferred_element_type=jnp.float32,
    )
    return jnp.where(irrep_ij[:, None] == irrep_ab[None, :], summed, 0.0)


def solution(mesh):
    n_row, n_col = mesh.shape["row"], mesh.shape["col"]

    def body(*arrays):
        amplitudes, integrals, irrep_ij, irrep_ab, irrep_cd = arrays
        arrays = (
            amplitudes, integrals, irrep_ij.reshape(1, -1), irrep_ab.reshape(1, -1),
            irrep_cd.reshape(n_row, -1),
        )
        if n_col % n_row or n_col % 2:
            return dense_ladder(n_row, n_col, *arrays)
        ladder, fits, *arrays = packed_ladder(n_row, n_col, *arrays)
        return lax.cond(
            fits[0] == 1,
            lambda ladder, *_: ladder, lambda _, *rest: dense_ladder(n_row, n_col, *rest),
            ladder, *arrays,
        )

    in_specs = (P("row", "col"), P("col", "row"), P("row"), P("col"), P())
    return jax.shard_map(
        body, mesh=mesh, in_specs=in_specs, out_specs=P("row", "col"), check_vma=False
    )
```

```python
import functools
import math

import jax
import jax.numpy as jnp
from jax import lax
from jax.experimental import pallas as pl
from jax.experimental.pallas import tpu as pltpu
from jax.sharding import PartitionSpec as P

N_IRREP = 8
MESH = pl.DeviceIdType.MESH


def slots_for(block):
    need = block / N_IRREP + 4.0 * math.sqrt(block * (N_IRREP - 1)) / N_IRREP
    return min(-(-block // 8) * 8, 8 * math.ceil(need / 8))


def halves(x):
    high = x.astype(jnp.bfloat16)
    low = (x - high.astype(jnp.float32)).astype(jnp.bfloat16)
    return high, low


def nt_dot(a, b):
    return lax.dot_general(a, b, (((1,), (1,)), ((), ())), preferred_element_type=jnp.float32)


def selector(labels, slots):
    block = labels.shape[1]
    irreps = lax.broadcasted_iota(jnp.int32, (N_IRREP, block), 0)
    member = jnp.where(irreps == labels, 1.0, 0.0)
    before = lax.broadcasted_iota(jnp.int32, (block, block), 0) < lax.broadcasted_iota(
        jnp.int32, (block, block), 1
    )
    earlier = jnp.dot(
        member.astype(jnp.bfloat16),
        jnp.where(before, 1.0, 0.0).astype(jnp.bfloat16),
        preferred_element_type=jnp.float32,
    )
    rank = jnp.sum(member * earlier, axis=0, keepdims=True)
    place = labels * slots + rank.astype(jnp.int32)
    rows = lax.broadcasted_iota(jnp.int32, (N_IRREP * slots, block), 0)
    return jnp.where(rows == place, 1.0, 0.0).astype(jnp.bfloat16)


def pack(sel, values, labels, slots):
    high, low = halves(values)
    picked = nt_dot(
        jnp.concatenate([sel, sel], axis=1), jnp.concatenate([high, low], axis=1)
    )
    packed = jnp.zeros((slots, values.shape[0]), jnp.float32)
    for irrep in range(N_IRREP):
        packed = jnp.where(
            labels == irrep, picked[irrep * slots : (irrep + 1) * slots], packed
        )
    return packed


def kernel(
    n_row, n_col, slots, amp_hbm, int_hbm, ij_hbm, ab_hbm, cd_hbm, out_ref, fits_ref,
    amp_ref, int_ref, ij_ref, ab_ref, cd_ref, t_all, v_all,
    load, ready, v_ready, t_send, t_recv, v_send, v_recv,
):
    row, col = lax.axis_index("row"), lax.axis_index("col")
    per_row = n_col // n_row
    ij_rows, part = amp_ref.shape
    block = int_ref.shape[1]
    odd = lax.rem(col, 2) == 1

    barrier = pltpu.get_barrier_semaphore()

    def greet(*device):
        pl.semaphore_signal(barrier, inc=1, device_id=device, device_id_type=MESH)

    row_peers = [lax.rem(row + step, n_row) for step in range(1, n_row)]
    for step in range(1, n_row):
        pl.when(row + step < n_row)(lambda: greet(row + step, col))
    for step in range(1, n_col):
        pl.when(col + step < n_col)(lambda: greet(row, col + step))
    pl.when(odd)(lambda: greet(row, col - 1))

    loads = [
        pltpu.make_async_copy(source, target, load.at[place])
        for place, (source, target) in enumerate(
            ((cd_hbm, cd_ref), (ij_hbm, ij_ref), (amp_hbm, amp_ref), (ab_hbm, ab_ref), (int_hbm, int_ref))
        )
    ]
    for copy in loads:
        copy.start()
    pl.semaphore_wait(barrier, row + col + jnp.where(odd, 0, 1))

    def tell(peer):
        pl.semaphore_signal(
            ready.at[col], inc=1, device_id=(row, peer), device_id_type=MESH
        )

    for step in reversed(range(1, n_col)):
        far = jnp.logical_or(step > 1, jnp.logical_not(odd))
        pl.when(jnp.logical_and(col >= step, far))(lambda: tell(col - step))

    def tell_row(peer):
        pl.semaphore_signal(
            v_ready.at[row], inc=1, device_id=(peer, col), device_id_type=MESH
        )

    for step in range(1, n_row):
        pl.when(row >= step)(lambda: tell_row(row - step))
    for copy in loads[:3]:
        copy.wait()

    t_sel = selector(cd_ref[pl.ds(lax.div(col, per_row), 1), :], slots)
    amps = amp_ref[...]
    if per_row > 1:
        lanes = lax.broadcasted_iota(jnp.int32, (ij_rows, block), 1)
        own = lax.div(lanes, part) == lax.rem(col, per_row)
        amps = jnp.where(own, jnp.concatenate([amps] * per_row, axis=1), 0.0)
    t_all[col] = pack(t_sel, amps, ij_ref[...], slots)

    def t_copy(origin, peer):
        return pltpu.make_async_remote_copy(
            src_ref=t_all.at[origin], dst_ref=t_all.at[origin],
            send_sem=t_send.at[peer], recv_sem=t_recv.at[origin],
            device_id=(row, peer), device_id_type=MESH,
        )

    for step in reversed(range(1, n_col)):
        pl.when(col >= step)(lambda: t_copy(col, col - step).start())
    pl.when(jnp.logical_not(odd))(lambda: t_copy(col, col + 1).start())

    v_sel = selector(cd_ref[pl.ds(row, 1), :], slots)
    for copy in loads[3:]:
        copy.wait()
    v_all[row] = pack(v_sel, int_ref[...], ab_ref[...], slots)

    def v_copy(origin, peer):
        return pltpu.make_async_remote_copy(
            src_ref=v_all.at[origin], dst_ref=v_all.at[origin],
            send_sem=v_send.at[peer], recv_sem=v_recv.at[origin],
            device_id=(peer, col), device_id_type=MESH,
        )

    for step in reversed(range(1, n_row)):
        pl.when(row >= step)(lambda: v_copy(row, row - step).start())
    for step in range(1, n_row):

        @pl.when(row + step < n_row)
        def _():
            pl.semaphore_wait(v_ready.at[row + step], 1)
            v_copy(row, row + step).start()

    for step in range(1, n_col):
        far = jnp.logical_or(step > 1, odd)

        @pl.when(jnp.logical_and(col + step < n_col, far))
        def _():
            pl.semaphore_wait(ready.at[col + step], 1)
            t_copy(col, col + step).start()

    most = jnp.zeros((n_row, 1), jnp.int32)
    for irrep in range(N_IRREP):
        count = jnp.sum(jnp.where(cd_ref[...] == irrep, 1, 0), axis=1, keepdims=True)
        most = jnp.maximum(most, count)
    fits_ref[0] = jnp.where(jnp.max(most) <= slots, 1, 0)
    wide = jnp.broadcast_to(ij_ref[...], (8, ij_rows)).astype(jnp.float32)
    ij_column = jnp.transpose(wide)[:, :1].astype(jnp.int32)
    same = ij_column == ab_ref[...]

    for step in range(1, n_col):
        pl.when(col + step < n_col)(lambda: t_copy(col + step, col).wait_recv())
    for step in range(1, n_col):
        pl.when(col >= step)(lambda: t_copy(col - step, col).wait_recv())
    t_rows = []
    for first in range(0, n_col, per_row):
        total = t_all[first]
        for other in range(first + 1, first + per_row):
            total = total + t_all[other]
        t_rows.append(total)
    t_high, t_low = halves(jnp.transpose(jnp.concatenate(t_rows, axis=0)))
    left = jnp.concatenate([t_high, t_high, t_low], axis=1)

    for peer in row_peers:
        v_copy(peer, row).wait_recv()
    v_high, v_low = halves(v_all[...].reshape(n_row * slots, -1))
    right = jnp.concatenate([v_high, v_low, v_high], axis=0)
    summed = jnp.dot(left, right, preferred_element_type=jnp.float32)
    out_ref[...] = jnp.where(same, summed, 0.0)

    for peer in row_peers:
        v_copy(row, peer).wait_send()
    for step in range(1, n_col):
        pl.when(col >= step)(lambda: t_copy(col, col - step).wait_send())
        pl.when(col + step < n_col)(lambda: t_copy(col, col + step).wait_send())


def packed_ladder(n_row, n_col, amplitudes, integrals, irrep_ij, irrep_ab, irrep_cd):
    ij_rows, ab_rows = amplitudes.shape[0], integrals.shape[0]
    block = integrals.shape[1]
    slots = slots_for(block)
    vmem = pl.BlockSpec(memory_space=pltpu.VMEM)
    operands = (amplitudes, integrals, irrep_ij, irrep_ab, irrep_cd)
    return pl.pallas_call(
        functools.partial(kernel, n_row, n_col, slots),
        out_shape=(
            jax.ShapeDtypeStruct((ij_rows, ab_rows), jnp.float32),
            jax.ShapeDtypeStruct((1,), jnp.int32),
        ) + tuple(jax.ShapeDtypeStruct(array.shape, array.dtype) for array in operands),
        in_specs=[pl.BlockSpec(memory_space=pltpu.HBM)] * 5,
        out_specs=(vmem, pl.BlockSpec(memory_space=pltpu.SMEM)) + (vmem,) * 5,
        scratch_shapes=[
            pltpu.VMEM((n_col, slots, ij_rows), jnp.float32),
            pltpu.VMEM((n_row, slots, ab_rows), jnp.float32),
            pltpu.SemaphoreType.DMA((5,)),
            pltpu.SemaphoreType.REGULAR((n_col,)),
            pltpu.SemaphoreType.REGULAR((n_row,)),
            pltpu.SemaphoreType.DMA((n_col,)),
            pltpu.SemaphoreType.DMA((n_col,)),
            pltpu.SemaphoreType.DMA((n_row,)),
            pltpu.SemaphoreType.DMA((n_row,)),
        ],
        compiler_params=pltpu.CompilerParams(
            collective_id=0, has_side_effects=True, vmem_limit_bytes=60 * 1024 * 1024
        ),
    )(*operands)


def gather_kernel(
    n_row, n_col, amp_ref, int_ref, ij_ref, ab_ref, cd_ref, t_all, v_all, ij_out, ab_out, cd_out,
    t_send, t_recv, v_send, v_recv, own,
):
    row, col = lax.axis_index("row"), lax.axis_index("col")
    barrier = pltpu.get_barrier_semaphore()

    def with_row(step):
        return (lax.rem(row + step, n_row), col)

    def with_col(step):
        return (row, lax.rem(col + step, n_col))

    for peer_of, peers in ((with_row, n_row), (with_col, n_col)):

        @pl.loop(1, peers)
        def _(step):
            pl.semaphore_signal(barrier, inc=1, device_id=peer_of(step), device_id_type=MESH)

    kept = [
        pltpu.make_async_copy(int_ref, v_all.at[row], own.at[0]),
        pltpu.make_async_copy(amp_ref, t_all.at[col], own.at[1]),
        pltpu.make_async_copy(ij_ref, ij_out, own.at[2]),
        pltpu.make_async_copy(ab_ref, ab_out, own.at[3]),
        pltpu.make_async_copy(cd_ref, cd_out, own.at[4]),
    ]
    for copy in kept:
        copy.start()
    pl.semaphore_wait(barrier, n_row - 1 + n_col - 1)

    def v_copy(step, source):
        return pltpu.make_async_remote_copy(
            src_ref=int_ref, dst_ref=v_all.at[source],
            send_sem=v_send.at[step], recv_sem=v_recv.at[source],
            device_id=with_row(step), device_id_type=MESH,
        )

    def t_copy(step, source):
        return pltpu.make_async_remote_copy(
            src_ref=amp_ref, dst_ref=t_all.at[source],
            send_sem=t_send.at[step], recv_sem=t_recv.at[source],
            device_id=with_col(step), device_id_type=MESH,
        )

    for copy_of, me, peers in ((v_copy, row, n_row), (t_copy, col, n_col)):

        @pl.loop(1, peers)
        def _(step):
            copy_of(step, me).start()

    for copy_of, me, peers in ((v_copy, row, n_row), (t_copy, col, n_col)):

        @pl.loop(1, peers)
        def _(step):
            copy_of(step, me).wait_send()
            copy_of(step, lax.rem(me + step, peers)).wait_recv()

    for copy in kept:
        copy.wait()


def dense_ladder(n_row, n_col, amplitudes, integrals, irrep_ij, irrep_ab, irrep_cd):
    vmem = pl.BlockSpec(memory_space=pltpu.VMEM)
    labels = (irrep_ij, irrep_ab, irrep_cd)
    t_all, v_all, irrep_ij, irrep_ab, irrep_cd = pl.pallas_call(
        functools.partial(gather_kernel, n_row, n_col),
        out_shape=(
            jax.ShapeDtypeStruct((n_col,) + amplitudes.shape, amplitudes.dtype),
            jax.ShapeDtypeStruct((n_row,) + integrals.shape, integrals.dtype),
        ) + tuple(jax.ShapeDtypeStruct(label.shape, label.dtype) for label in labels),
        in_specs=[pl.BlockSpec(memory_space=pltpu.HBM)] * 5,
        out_specs=(vmem,) * 5,
        scratch_shapes=[
            pltpu.SemaphoreType.DMA((n_col,)),
            pltpu.SemaphoreType.DMA((n_col,)),
            pltpu.SemaphoreType.DMA((n_row,)),
            pltpu.SemaphoreType.DMA((n_row,)),
            pltpu.SemaphoreType.DMA((5,)),
        ],
        compiler_params=pltpu.CompilerParams(
            collective_id=1, has_side_effects=True, vmem_limit_bytes=32 * 1024 * 1024
        ),
    )(amplitudes, integrals, *labels)
    irrep_ij, irrep_ab, irrep_cd = (label.reshape(-1) for label in (irrep_ij, irrep_ab, irrep_cd))
    amps = jnp.swapaxes(t_all, 0, 1).reshape(amplitudes.shape[0], -1)
    ints = jnp.swapaxes(v_all, 0, 1).reshape(integrals.shape[0], -1)
    masked = jnp.where(irrep_ij[:, None] == irrep_cd[None, :], amps, 0.0)
    summed = lax.dot_general(
        masked, ints, (((1,), (1,)), ((), ())),
        precision=lax.Precision.HIGHEST, preferred_element_type=jnp.float32,
    )
    return jnp.where(irrep_ij[:, None] == irrep_ab[None, :], summed, 0.0)


def solution(mesh):
    n_row, n_col = mesh.shape["row"], mesh.shape["col"]

    def body(*arrays):
        amplitudes, integrals, irrep_ij, irrep_ab, irrep_cd = arrays
        arrays = (
            amplitudes, integrals, irrep_ij.reshape(1, -1), irrep_ab.reshape(1, -1),
            irrep_cd.reshape(n_row, -1),
        )
        if n_col % n_row or n_col % 2:
            return dense_ladder(n_row, n_col, *arrays)
        ladder, fits, *arrays = packed_ladder(n_row, n_col, *arrays)
        return lax.cond(
            fits[0] == 1,
            lambda ladder, *_: ladder, lambda _, *rest: dense_ladder(n_row, n_col, *rest),
            ladder, *arrays,
        )

    in_specs = (P("row", "col"), P("col", "row"), P("row"), P("col"), P())
    return jax.shard_map(
        body, mesh=mesh, in_specs=in_specs, out_specs=P("row", "col"), check_vma=False
    )
```

```python
import functools
import math

import jax
import jax.numpy as jnp
from jax import lax
from jax.experimental import pallas as pl
from jax.experimental.pallas import tpu as pltpu
from jax.sharding import PartitionSpec as P

N_IRREP = 8
MESH = pl.DeviceIdType.MESH


def slots_for(block):
    need = block / N_IRREP + 4.0 * math.sqrt(block * (N_IRREP - 1)) / N_IRREP
    return min(-(-block // 8) * 8, 8 * math.ceil(need / 8))


def halves(x):
    high = x.astype(jnp.bfloat16)
    low = (x - high.astype(jnp.float32)).astype(jnp.bfloat16)
    return high, low


def nt_dot(a, b):
    return lax.dot_general(a, b, (((1,), (1,)), ((), ())), preferred_element_type=jnp.float32)


def selector(labels, slots):
    block = labels.shape[1]
    irreps = lax.broadcasted_iota(jnp.int32, (N_IRREP, block), 0)
    member = jnp.where(irreps == labels, 1.0, 0.0)
    before = lax.broadcasted_iota(jnp.int32, (block, block), 0) < lax.broadcasted_iota(
        jnp.int32, (block, block), 1
    )
    earlier = jnp.dot(
        member.astype(jnp.bfloat16),
        jnp.where(before, 1.0, 0.0).astype(jnp.bfloat16),
        preferred_element_type=jnp.float32,
    )
    rank = jnp.sum(member * earlier, axis=0, keepdims=True)
    place = labels * slots + rank.astype(jnp.int32)
    rows = lax.broadcasted_iota(jnp.int32, (N_IRREP * slots, block), 0)
    return jnp.where(rows == place, 1.0, 0.0).astype(jnp.bfloat16)


def pack(sel, values, labels, slots):
    high, low = halves(values)
    picked = nt_dot(
        jnp.concatenate([sel, sel], axis=1), jnp.concatenate([high, low], axis=1)
    )
    packed = jnp.zeros((slots, values.shape[0]), jnp.float32)
    for irrep in range(N_IRREP):
        packed = jnp.where(
            labels == irrep, picked[irrep * slots : (irrep + 1) * slots], packed
        )
    return packed


def kernel(
    n_row, n_col, slots, amp_hbm, int_hbm, ij_hbm, ab_hbm, cd_hbm, out_ref, fits_ref,
    amp_ref, int_ref, ij_ref, ab_ref, cd_ref, t_all, v_all,
    load, ready, v_ready, t_send, t_recv, v_send, v_recv,
):
    row, col = lax.axis_index("row"), lax.axis_index("col")
    per_row = n_col // n_row
    ij_rows, part = amp_ref.shape
    block = int_ref.shape[1]
    odd = lax.rem(col, 2) == 1

    loads = [
        pltpu.make_async_copy(source, target, load.at[place])
        for place, (source, target) in enumerate(
            ((cd_hbm, cd_ref), (ij_hbm, ij_ref), (amp_hbm, amp_ref), (ab_hbm, ab_ref), (int_hbm, int_ref))
        )
    ]
    for copy in loads:
        copy.start()

    barrier = pltpu.get_barrier_semaphore()

    def greet(*device):
        pl.semaphore_signal(barrier, inc=1, device_id=device, device_id_type=MESH)

    row_peers = [lax.rem(row + step, n_row) for step in range(1, n_row)]
    for step in range(1, n_row):
        pl.when(row + step < n_row)(lambda: greet(row + step, col))
    for step in range(1, n_col):
        pl.when(col + step < n_col)(lambda: greet(row, col + step))
    pl.when(odd)(lambda: greet(row, col - 1))

    pl.semaphore_wait(barrier, row + col + jnp.where(odd, 0, 1))

    def tell(peer):
        pl.semaphore_signal(
            ready.at[col], inc=1, device_id=(row, peer), device_id_type=MESH
        )

    for step in reversed(range(1, n_col)):
        far = jnp.logical_or(step > 1, jnp.logical_not(odd))
        pl.when(jnp.logical_and(col >= step, far))(lambda: tell(col - step))

    def tell_row(peer):
        pl.semaphore_signal(
            v_ready.at[row], inc=1, device_id=(peer, col), device_id_type=MESH
        )

    for step in range(1, n_row):
        pl.when(row >= step)(lambda: tell_row(row - step))
    for copy in loads[:3]:
        copy.wait()

    t_sel = selector(cd_ref[pl.ds(lax.div(col, per_row), 1), :], slots)
    amps = amp_ref[...]
    if per_row > 1:
        lanes = lax.broadcasted_iota(jnp.int32, (ij_rows, block), 1)
        own = lax.div(lanes, part) == lax.rem(col, per_row)
        amps = jnp.where(own, jnp.concatenate([amps] * per_row, axis=1), 0.0)
    t_all[col] = pack(t_sel, amps, ij_ref[...], slots)

    def t_copy(origin, peer):
        return pltpu.make_async_remote_copy(
            src_ref=t_all.at[origin], dst_ref=t_all.at[origin],
            send_sem=t_send.at[peer], recv_sem=t_recv.at[origin],
            device_id=(row, peer), device_id_type=MESH,
        )

    for step in reversed(range(1, n_col)):
        pl.when(col >= step)(lambda: t_copy(col, col - step).start())
    pl.when(jnp.logical_not(odd))(lambda: t_copy(col, col + 1).start())

    v_sel = selector(cd_ref[pl.ds(row, 1), :], slots)
    for copy in loads[3:]:
        copy.wait()
    v_all[row] = pack(v_sel, int_ref[...], ab_ref[...], slots)

    def v_copy(origin, peer):
        return pltpu.make_async_remote_copy(
            src_ref=v_all.at[origin], dst_ref=v_all.at[origin],
            send_sem=v_send.at[peer], recv_sem=v_recv.at[origin],
            device_id=(peer, col), device_id_type=MESH,
        )

    for step in reversed(range(1, n_row)):
        pl.when(row >= step)(lambda: v_copy(row, row - step).start())
    for step in range(1, n_row):

        @pl.when(row + step < n_row)
        def _():
            pl.semaphore_wait(v_ready.at[row + step], 1)
            v_copy(row, row + step).start()

    for step in range(1, n_col):
        far = jnp.logical_or(step > 1, odd)

        @pl.when(jnp.logical_and(col + step < n_col, far))
        def _():
            pl.semaphore_wait(ready.at[col + step], 1)
            t_copy(col, col + step).start()

    most = jnp.zeros((n_row, 1), jnp.int32)
    for irrep in range(N_IRREP):
        count = jnp.sum(jnp.where(cd_ref[...] == irrep, 1, 0), axis=1, keepdims=True)
        most = jnp.maximum(most, count)
    fits_ref[0] = jnp.where(jnp.max(most) <= slots, 1, 0)
    wide = jnp.broadcast_to(ij_ref[...], (8, ij_rows)).astype(jnp.float32)
    ij_column = jnp.transpose(wide)[:, :1].astype(jnp.int32)
    same = ij_column == ab_ref[...]

    for step in range(1, n_col):
        pl.when(col + step < n_col)(lambda: t_copy(col + step, col).wait_recv())
    for step in range(1, n_col):
        pl.when(col >= step)(lambda: t_copy(col - step, col).wait_recv())
    t_rows = []
    for first in range(0, n_col, per_row):
        total = t_all[first]
        for other in range(first + 1, first + per_row):
            total = total + t_all[other]
        t_rows.append(total)
    t_high, t_low = halves(jnp.transpose(jnp.concatenate(t_rows, axis=0)))
    left = jnp.concatenate([t_high, t_high, t_low], axis=1)

    for peer in row_peers:
        v_copy(peer, row).wait_recv()
    v_high, v_low = halves(v_all[...].reshape(n_row * slots, -1))
    right = jnp.concatenate([v_high, v_low, v_high], axis=0)
    summed = jnp.dot(left, right, preferred_element_type=jnp.float32)
    out_ref[...] = jnp.where(same, summed, 0.0)

    for peer in row_peers:
        v_copy(row, peer).wait_send()
    for step in range(1, n_col):
        pl.when(col >= step)(lambda: t_copy(col, col - step).wait_send())
        pl.when(col + step < n_col)(lambda: t_copy(col, col + step).wait_send())


def packed_ladder(n_row, n_col, amplitudes, integrals, irrep_ij, irrep_ab, irrep_cd):
    ij_rows, ab_rows = amplitudes.shape[0], integrals.shape[0]
    block = integrals.shape[1]
    slots = slots_for(block)
    vmem = pl.BlockSpec(memory_space=pltpu.VMEM)
    operands = (amplitudes, integrals, irrep_ij, irrep_ab, irrep_cd)
    return pl.pallas_call(
        functools.partial(kernel, n_row, n_col, slots),
        out_shape=(
            jax.ShapeDtypeStruct((ij_rows, ab_rows), jnp.float32),
            jax.ShapeDtypeStruct((1,), jnp.int32),
        ) + tuple(jax.ShapeDtypeStruct(array.shape, array.dtype) for array in operands),
        in_specs=[pl.BlockSpec(memory_space=pltpu.HBM)] * 5,
        out_specs=(vmem, pl.BlockSpec(memory_space=pltpu.SMEM)) + (vmem,) * 5,
        scratch_shapes=[
            pltpu.VMEM((n_col, slots, ij_rows), jnp.float32),
            pltpu.VMEM((n_row, slots, ab_rows), jnp.float32),
            pltpu.SemaphoreType.DMA((5,)),
            pltpu.SemaphoreType.REGULAR((n_col,)),
            pltpu.SemaphoreType.REGULAR((n_row,)),
            pltpu.SemaphoreType.DMA((n_col,)),
            pltpu.SemaphoreType.DMA((n_col,)),
            pltpu.SemaphoreType.DMA((n_row,)),
            pltpu.SemaphoreType.DMA((n_row,)),
        ],
        compiler_params=pltpu.CompilerParams(
            collective_id=0, has_side_effects=True, vmem_limit_bytes=60 * 1024 * 1024
        ),
    )(*operands)


def gather_kernel(
    n_row, n_col, amp_ref, int_ref, ij_ref, ab_ref, cd_ref, t_all, v_all, ij_out, ab_out, cd_out,
    t_send, t_recv, v_send, v_recv, own,
):
    row, col = lax.axis_index("row"), lax.axis_index("col")
    barrier = pltpu.get_barrier_semaphore()

    def with_row(step):
        return (lax.rem(row + step, n_row), col)

    def with_col(step):
        return (row, lax.rem(col + step, n_col))

    for peer_of, peers in ((with_row, n_row), (with_col, n_col)):

        @pl.loop(1, peers)
        def _(step):
            pl.semaphore_signal(barrier, inc=1, device_id=peer_of(step), device_id_type=MESH)

    kept = [
        pltpu.make_async_copy(int_ref, v_all.at[row], own.at[0]),
        pltpu.make_async_copy(amp_ref, t_all.at[col], own.at[1]),
        pltpu.make_async_copy(ij_ref, ij_out, own.at[2]),
        pltpu.make_async_copy(ab_ref, ab_out, own.at[3]),
        pltpu.make_async_copy(cd_ref, cd_out, own.at[4]),
    ]
    for copy in kept:
        copy.start()
    pl.semaphore_wait(barrier, n_row - 1 + n_col - 1)

    def v_copy(step, source):
        return pltpu.make_async_remote_copy(
            src_ref=int_ref, dst_ref=v_all.at[source],
            send_sem=v_send.at[step], recv_sem=v_recv.at[source],
            device_id=with_row(step), device_id_type=MESH,
        )

    def t_copy(step, source):
        return pltpu.make_async_remote_copy(
            src_ref=amp_ref, dst_ref=t_all.at[source],
            send_sem=t_send.at[step], recv_sem=t_recv.at[source],
            device_id=with_col(step), device_id_type=MESH,
        )

    for copy_of, me, peers in ((v_copy, row, n_row), (t_copy, col, n_col)):

        @pl.loop(1, peers)
        def _(step):
            copy_of(step, me).start()

    for copy_of, me, peers in ((v_copy, row, n_row), (t_copy, col, n_col)):

        @pl.loop(1, peers)
        def _(step):
            copy_of(step, me).wait_send()
            copy_of(step, lax.rem(me + step, peers)).wait_recv()

    for copy in kept:
        copy.wait()


def dense_ladder(n_row, n_col, amplitudes, integrals, irrep_ij, irrep_ab, irrep_cd):
    vmem = pl.BlockSpec(memory_space=pltpu.VMEM)
    labels = (irrep_ij, irrep_ab, irrep_cd)
    t_all, v_all, irrep_ij, irrep_ab, irrep_cd = pl.pallas_call(
        functools.partial(gather_kernel, n_row, n_col),
        out_shape=(
            jax.ShapeDtypeStruct((n_col,) + amplitudes.shape, amplitudes.dtype),
            jax.ShapeDtypeStruct((n_row,) + integrals.shape, integrals.dtype),
        ) + tuple(jax.ShapeDtypeStruct(label.shape, label.dtype) for label in labels),
        in_specs=[pl.BlockSpec(memory_space=pltpu.HBM)] * 5,
        out_specs=(vmem,) * 5,
        scratch_shapes=[
            pltpu.SemaphoreType.DMA((n_col,)),
            pltpu.SemaphoreType.DMA((n_col,)),
            pltpu.SemaphoreType.DMA((n_row,)),
            pltpu.SemaphoreType.DMA((n_row,)),
            pltpu.SemaphoreType.DMA((5,)),
        ],
        compiler_params=pltpu.CompilerParams(
            collective_id=1, has_side_effects=True, vmem_limit_bytes=32 * 1024 * 1024
        ),
    )(amplitudes, integrals, *labels)
    irrep_ij, irrep_ab, irrep_cd = (label.reshape(-1) for label in (irrep_ij, irrep_ab, irrep_cd))
    amps = jnp.swapaxes(t_all, 0, 1).reshape(amplitudes.shape[0], -1)
    ints = jnp.swapaxes(v_all, 0, 1).reshape(integrals.shape[0], -1)
    masked = jnp.where(irrep_ij[:, None] == irrep_cd[None, :], amps, 0.0)
    summed = lax.dot_general(
        masked, ints, (((1,), (1,)), ((), ())),
        precision=lax.Precision.HIGHEST, preferred_element_type=jnp.float32,
    )
    return jnp.where(irrep_ij[:, None] == irrep_ab[None, :], summed, 0.0)


def solution(mesh):
    n_row, n_col = mesh.shape["row"], mesh.shape["col"]

    def body(*arrays):
        amplitudes, integrals, irrep_ij, irrep_ab, irrep_cd = arrays
        arrays = (
            amplitudes, integrals, irrep_ij.reshape(1, -1), irrep_ab.reshape(1, -1),
            irrep_cd.reshape(n_row, -1),
        )
        if n_col % n_row or n_col % 2:
            return dense_ladder(n_row, n_col, *arrays)
        ladder, fits, *arrays = packed_ladder(n_row, n_col, *arrays)
        return lax.cond(
            fits[0] == 1,
            lambda ladder, *_: ladder, lambda _, *rest: dense_ladder(n_row, n_col, *rest),
            ladder, *arrays,
        )

    in_specs = (P("row", "col"), P("col", "row"), P("row"), P("col"), P())
    return jax.shard_map(
        body, mesh=mesh, in_specs=in_specs, out_specs=P("row", "col"), check_vma=False
    )
```
